32 devices in a mesh: ctx: 16 (over z, x, core), fsdp: 2 (over y).
Axes of the slice: x: 2, y: 2, z: 4, core: 2. Of those that a mesh axis runs over, the one named last changes fastest.
Arguments:
- tokens: bfloat16 [4, 1024, 576], P('fsdp', 'ctx'), may hold values from -6 to 6
- query_matrix: bfloat16 [576, 576], P('fsdp'), may hold values from -0.25 to 0.25
- key_projection: bfloat16 [576, 192], P('fsdp'), may hold values from -0.25 to 0.25
- value_projection: bfloat16 [576, 192], P('fsdp'), may hold values from -0.25 to 0.25
- output_matrix: bfloat16 [576, 576], P('fsdp'), may hold values from -2 to 2
- attn_gain: bfloat16 [576], P('fsdp'), may hold values from 0.099609375 to 1.8984375
- mlp_gain: bfloat16 [576], P('fsdp'), may hold values from 0.099609375 to 1.8984375
- gate_matrix: bfloat16 [576, 1536], P(None, 'fsdp'), may hold values from -0.25 to 0.25
- up_matrix: bfloat16 [576, 1536], P(None, 'fsdp'), may hold values from -0.25 to 0.25
- down_matrix: bfloat16 [1536, 576], P('fsdp'), may hold values from -0.15625 to 0.15625
- pair_table: int32 [16, 2], replicated, may hold values from 0 to 31, as said below
- doc_ids: int32 [4, 1024], P('fsdp'), may hold values from 0 to 15, never falling along the last dimension, each value on 1 to 128 neighbouring positions
- out_grad: bfloat16 [4, 1024, 576], P('fsdp', 'ctx'), may hold values from -6 to 6
Outputs:
- block_out: bfloat16 [4, 1024, 576], P('fsdp', 'ctx')
- input_grad: float32 [4, 1024, 576], P('fsdp', 'ctx')
- query_grad: float32 [576, 576], P('fsdp')
- key_grad: float32 [576, 192], P('fsdp')
- value_grad: float32 [576, 192], P('fsdp')
- output_grad: float32 [576, 576], P('fsdp')
- attn_gain_grad: float32 [576], P('fsdp')
- mlp_gain_grad: float32 [576], P('fsdp')
- gate_grad: float32 [576, 1536], P(None, 'fsdp')
- up_grad: float32 [576, 1536], P(None, 'fsdp')
- down_grad: float32 [1536, 576], P('fsdp')
The draws below stay inside these ranges and needn't reach their ends.
Inputs may be any that keep to these rules, and one draw needn't show every extreme that they name: `pair_table`: row i holds a block number b below 16 and then its mirror 2 * 16 - 1 - b; the first entries of the rows are each of 0 to 15 once. `doc_ids`: document ids never fall along a sequence; every id of 0 to 15 appears, each document holds 1 to 128 positions, and one holds exactly 128.
All inputs are finite; a program needn't handle non-finite values.
Results may differ from the reference program's by a relative error of at most 0.02.
Values may be sent and summed in bfloat16 or wider, within the bound.
A program may use at most 192 MiB of HBM per device.

```python
import math
import jax
import jax.numpy as jnp
import numpy as np
from jax import lax

MODEL_WIDTH = 576
QUERY_HEADS = 9
KEY_VALUE_HEADS = 3
HEAD_SIZE = 64
FF = 1536
TOK_DEV = 64
DOCS = 16
BLOCKS = 32
BLOCK = 32
SEQUENCE_LENGTH = 1024
SEQS = 4


def draw_pair_table(key, part):
    half = BLOCKS // 2
    order = jax.random.permutation(key, half).astype(jnp.int32)
    return jnp.stack([order, BLOCKS - 1 - order], axis=1).astype(jnp.int32)


def block_levels(rng, dims, shards, smallest, top_value):
    loudness, own = 1.0, jax.random.fold_in(rng, 6)
    for axis_at, shards_of in shards:
        steps = jnp.exp(jax.random.uniform(jax.random.fold_in(own, axis_at), (shards_of,), jnp.float32, smallest / len(shards), top_value / len(shards)))
        loudness = loudness * jnp.repeat(steps, dims[axis_at] // shards_of).reshape([-1 if axis == axis_at else 1 for axis in range(len(dims))])
    return loudness


def split_up(count, total, reach, slope):
    weights = [(1 << 20) // math.isqrt(standing ** slope) + 1 for standing in range(2, count + 1)]
    spare, counts = total - reach - (count - 1), [1] * (count - 1)
    while spare > 0:
        free = [i for i in range(count - 1) if counts[i] < reach]
        whole, left = sum([weights[i] for i in free]), spare
        for i in free:
            extra = min(reach - counts[i], max(1, left * weights[i] // whole), spare)
            counts[i] = counts[i] + extra
            spare = spare - extra
    return np.array([reach] + counts)


def ragged_sizes(rng, amount, total, most, lean):
    if amount == 2:
        one = jax.random.randint(rng, (), max(1, total - most), min(most, total - 1) + 1)
        return jnp.stack([one, total - one])
    sizes = jnp.asarray(split_up(amount, total, most, lean), jnp.int32)
    pairs = (amount - 1) // 2
    donor, taker = sizes[1:1 + 2 * pairs:2], sizes[2:2 + 2 * pairs:2]
    margin = jnp.minimum(donor - 1, most - taker)
    shifted = jax.random.randint(jax.random.fold_in(rng, 1), (pairs,), 0, 1 << 20) % (margin + 1)
    sizes = sizes.at[1:1 + 2 * pairs:2].set(donor - shifted).at[2:2 + 2 * pairs:2].set(taker + shifted)
    return sizes[jax.random.permutation(jax.random.fold_in(rng, 2), amount)]


def normal_values(key, extent, scale, most, shards=(), kind=jnp.bfloat16):
    entries = jax.random.normal(key, extent, jnp.float32) * scale
    if len(shards) > 0:
        entries = block_levels(key, extent, shards, -0.22, 0.18) * entries
    return jnp.clip(entries, min=-most, max=most).astype(kind)


def setup_inputs(seed: int = 0) -> dict:
    key_list = jax.random.split(jax.random.key(seed), 14)
    tokens = normal_values(key_list[0], (SEQS, SEQUENCE_LENGTH, MODEL_WIDTH), 1.0, 6.0, ((0, 2), (1, 16)))
    query_matrix = normal_values(key_list[1], (MODEL_WIDTH, QUERY_HEADS * HEAD_SIZE), MODEL_WIDTH ** -0.5, 0.25, ((0, 2),))
    key_projection = normal_values(key_list[2], (MODEL_WIDTH, KEY_VALUE_HEADS * HEAD_SIZE), MODEL_WIDTH ** -0.5, 0.25, ((0, 2),))
    value_projection = normal_values(key_list[3], (MODEL_WIDTH, KEY_VALUE_HEADS * HEAD_SIZE), MODEL_WIDTH ** -0.5, 0.25, ((0, 2),))
    output_matrix = normal_values(key_list[4], (QUERY_HEADS * HEAD_SIZE, MODEL_WIDTH), (QUERY_HEADS * HEAD_SIZE // 64) ** -0.5, 2.0, ((0, 2),))
    attn_gain = jnp.clip(1.0 + 0.18 * jax.random.normal(key_list[5], (MODEL_WIDTH,), jnp.float32), 0.099609375, 1.8984375).astype(jnp.bfloat16)
    mlp_gain = jnp.clip(1.0 + 0.18 * jax.random.normal(key_list[6], (MODEL_WIDTH,), jnp.float32), 0.099609375, 1.8984375).astype(jnp.bfloat16)
    gate_matrix = normal_values(key_list[7], (MODEL_WIDTH, FF), MODEL_WIDTH ** -0.5, 0.25, ((1, 2),))
    up_matrix = normal_values(key_list[8], (MODEL_WIDTH, FF), MODEL_WIDTH ** -0.5, 0.25, ((1, 2),))
    down_matrix = normal_values(key_list[9], (FF, MODEL_WIDTH), FF ** -0.5, 0.15625, ((0, 2),))
    pair_table = draw_pair_table(jax.random.fold_in(key_list[13], 71), 0)
    doc_ids = jax.vmap(lambda own: jnp.searchsorted(jnp.cumsum(ragged_sizes(own, DOCS, SEQUENCE_LENGTH, SEQUENCE_LENGTH // 8, 0)), jnp.arange(SEQUENCE_LENGTH), side="right"))(jax.random.split(key_list[11], SEQS)).reshape((SEQS, SEQUENCE_LENGTH)).astype(jnp.int32)
    out_grad = normal_values(key_list[12], (SEQS, SEQUENCE_LENGTH, MODEL_WIDTH), 1.0, 6.0, ((0, 2), (1, 16)))
    return dict(tokens=tokens, query_matrix=query_matrix, key_projection=key_projection, value_projection=value_projection, output_matrix=output_matrix, attn_gain=attn_gain, mlp_gain=mlp_gain, gate_matrix=gate_matrix, up_matrix=up_matrix, down_matrix=down_matrix, pair_table=pair_table, doc_ids=doc_ids, out_grad=out_grad)


@jax.custom_vjp
def lower_bound(v):
    return lax.optimization_barrier(v.astype(jnp.bfloat16)).astype(jnp.float32)

@jax.custom_vjp
def low_back(v):
    return v

def low_keep(v):
    return (lower_bound(v), None)

def low_pass(kept, grad):
    return (grad,)

def back_keep(v):
    return (v, None)

def back_low(kept, grad):
    return (lower_bound(grad),)
lower_bound.defvjp(low_keep, low_pass)
low_back.defvjp(back_keep, back_low)
epsilon = 1e-05
theta_base = 10000.0
masked_logits = -1e+30

def dealt_positions(pair_table):
    row_count = jnp.arange(SEQUENCE_LENGTH, dtype=jnp.int32)
    device = row_count // TOK_DEV
    which = row_count % TOK_DEV // BLOCK
    return (pair_table[device, which] * BLOCK + row_count % BLOCK).astype(jnp.int32)

def rope_tables(token_positions):
    half = HEAD_SIZE // 2
    freq = theta_base ** (-jnp.arange(half, dtype=jnp.float32) * 2.0 / HEAD_SIZE)
    angles = token_positions.astype(jnp.float32)[:, None] * freq[None, :]
    cosine_table = jnp.concatenate([jnp.cos(angles), jnp.cos(angles)], axis=-1)
    sine_table = jnp.concatenate([jnp.sin(angles), jnp.sin(angles)], axis=-1)
    return (cosine_table[:, None, :], sine_table[:, None, :])

def rotary_apply(value_rows, cosine_table, sine_table):
    half = value_rows.shape[-1] // 2
    turned = jnp.concatenate([-value_rows[..., half:], value_rows[..., :half]], axis=-1)
    return value_rows * cosine_table + turned * sine_table

def rms_norm(value_rows, gain):
    inverse = lax.rsqrt(lax.optimization_barrier(jnp.mean(value_rows * value_rows, axis=-1, keepdims=True)) + epsilon)
    return value_rows * inverse * gain

def attention_layer(query_rows, key_rows, value_rows, token_positions, document_list):
    group_index = QUERY_HEADS // KEY_VALUE_HEADS
    row_count = math.gcd(512, SEQUENCE_LENGTH)
    scale = 1.0 / math.sqrt(HEAD_SIZE)
    query_block_list = query_rows.reshape(SEQUENCE_LENGTH // row_count, row_count, KEY_VALUE_HEADS, group_index, HEAD_SIZE)
    pos_blocks = token_positions.reshape(SEQUENCE_LENGTH // row_count, row_count)
    doc_blocks = document_list.reshape(SEQUENCE_LENGTH // row_count, row_count)

    @jax.checkpoint
    def one_block(item):
        query_part, pos_part, doc_part = item
        scores = jnp.einsum('qhgd,khd->hgqk', query_part, key_rows, precision=lax.Precision.HIGHEST) * scale
        scores = low_back(scores)
        allowed = (token_positions[None, :] <= pos_part[:, None]) & (document_list[None, :] == doc_part[:, None])
        scores = jnp.where(allowed[None, None], scores, masked_logits)
        top = lax.optimization_barrier(jnp.max(scores, axis=-1, keepdims=True))
        expo = jnp.exp(scores - top)
        probs = expo / lax.optimization_barrier(jnp.sum(expo, axis=-1, keepdims=True))
        mixed_heads = jnp.einsum('hgqk,khd->qhgd', lower_bound(probs), value_rows, precision=lax.Precision.HIGHEST)
        return mixed_heads.reshape(row_count, QUERY_HEADS * HEAD_SIZE)
    result = lax.map(one_block, (query_block_list, pos_blocks, doc_blocks))
    return result.reshape(SEQUENCE_LENGTH, QUERY_HEADS * HEAD_SIZE)

def layer(inputs, weights, token_positions, document_list):
    query_matrix, key_projection, value_projection, output_matrix, attn_gain, mlp_gain, gate_matrix, up_matrix, down_matrix = weights
    high = lax.Precision.HIGHEST
    cosine_table, sine_table = rope_tables(token_positions)
    hidden_one = lower_bound(rms_norm(inputs, attn_gain))
    query_lin = low_back(jnp.dot(hidden_one, query_matrix, precision=high))
    key_linear = low_back(jnp.dot(hidden_one, key_projection, precision=high))
    value_rows = lower_bound(low_back(jnp.dot(hidden_one, value_projection, precision=high)))
    query_rows = lower_bound(rotary_apply(query_lin.reshape(SEQUENCE_LENGTH, QUERY_HEADS, HEAD_SIZE), cosine_table, sine_table))
    key_rows = lower_bound(rotary_apply(key_linear.reshape(SEQUENCE_LENGTH, KEY_VALUE_HEADS, HEAD_SIZE), cosine_table, sine_table))
    mixed_heads = attention_layer(query_rows, key_rows, value_rows.reshape(SEQUENCE_LENGTH, KEY_VALUE_HEADS, HEAD_SIZE), token_positions, document_list)
    attn_in = lower_bound(low_back(mixed_heads))
    second = inputs + low_back(jnp.dot(attn_in, output_matrix, precision=high))
    hidden_two = lower_bound(rms_norm(second, mlp_gain))
    gate = low_back(jnp.dot(hidden_two, gate_matrix, precision=high))
    upper = low_back(jnp.dot(hidden_two, up_matrix, precision=high))
    activated = lower_bound(jax.nn.silu(gate) * upper)
    return second + low_back(jnp.dot(activated, down_matrix, precision=high))

def reference(tokens, query_matrix, key_projection, value_projection, output_matrix, attn_gain, mlp_gain, gate_matrix, up_matrix, down_matrix, pair_table, doc_ids, out_grad):
    token_positions = dealt_positions(pair_table)
    document_list = jnp.take(doc_ids, token_positions, axis=1)
    params = (query_matrix.astype(jnp.float32), key_projection.astype(jnp.float32), value_projection.astype(jnp.float32), output_matrix.astype(jnp.float32), attn_gain.astype(jnp.float32), mlp_gain.astype(jnp.float32), gate_matrix.astype(jnp.float32), up_matrix.astype(jnp.float32), down_matrix.astype(jnp.float32))

    def forward(inputs, weights):

        def one(carry, item):
            return (carry, layer(item[0], weights, token_positions, item[1]))
        carry, outputs = lax.scan(one, jnp.zeros((), jnp.float32), (inputs, document_list))
        return outputs
    outputs, pullback = jax.vjp(forward, tokens.astype(jnp.float32), params)
    input_grad, weight_grads = pullback(out_grad.astype(jnp.float32))
    query_grad, key_grad, value_grad, output_grad, attn_gain_grad, mlp_gain_grad, gate_grad, up_grad, down_grad = weight_grads
    return (outputs.astype(jnp.bfloat16), input_grad, query_grad, key_grad, value_grad, output_grad, attn_gain_grad, mlp_gain_grad, gate_grad, up_grad, down_grad)
```

```python
import functools
import math

import jax
import jax.numpy as jnp
from jax import lax
from jax.experimental import pallas as pl
from jax.experimental.pallas import tpu as pltpu
from jax.sharding import PartitionSpec as P

QUERY_HEADS = 9
KEY_VALUE_HEADS = 3
HEAD_SIZE = 64
GROUP = QUERY_HEADS // KEY_VALUE_HEADS
KV_WIDTH = KEY_VALUE_HEADS * HEAD_SIZE
SCALE = 1.0 / math.sqrt(HEAD_SIZE)

epsilon = 1e-05
theta_base = 10000.0
masked_logits = -1e30

VMEM = pl.BlockSpec(memory_space=pltpu.VMEM)
SMEM = pl.BlockSpec(memory_space=pltpu.SMEM)
MESH = pl.DeviceIdType.MESH
F32 = jnp.float32
BF16 = jnp.bfloat16


class Place:
    def __init__(self, members):
        self.members = members
        self.ctx = lax.axis_index("ctx")
        self.fsdp = lax.axis_index("fsdp")
        self.core = self.ctx % 2
        self.x = (self.ctx // 2) % 2
        self.far = self.ctx // 4

    def own(self, axis):
        return {"core": self.core, "x": self.x, "y": self.fsdp}[axis]

    def partner(self, axis):
        if axis == "core":
            return (self.ctx + 1 - 2 * self.core, self.fsdp)
        if axis == "x":
            return (self.ctx + 2 - 4 * self.x, self.fsdp)
        return (self.ctx, 1 - self.fsdp)

    def far_member(self, step):
        return (self.far + step) % self.members

    def far_device(self, step):
        return (self.far_member(step) * 4 + self.ctx % 4, self.fsdp)

    def greet(self, axes, far):
        barrier = pltpu.get_barrier_semaphore()
        for axis in axes:
            pl.semaphore_signal(barrier, inc=1, device_id=self.partner(axis), device_id_type=MESH)
        count = len(axes)
        if far:
            for step in range(1, self.members):
                pl.semaphore_signal(
                    barrier, inc=1, device_id=self.far_device(step), device_id_type=MESH
                )
            count += self.members - 1
        pl.semaphore_wait(barrier, count)


class Sems:
    def __init__(self, send, recv):
        self.send, self.recv, self.at = send, recv, 0

    def copy(self, src, dst, device):
        at = self.at
        self.at += 1
        made = pltpu.make_async_remote_copy(
            src_ref=src,
            dst_ref=dst,
            send_sem=self.send.at[at],
            recv_sem=self.recv.at[at],
            device_id=device,
            device_id_type=MESH,
        )
        made.start()
        return made


def params(collective_id):
    return pltpu.CompilerParams(
        collective_id=collective_id, has_side_effects=True, vmem_limit_bytes=60 * 2**20
    )


def weights_kernel(members, count, *refs):
    ins, gain_in = refs[:count], refs[count]
    outs, gain_out = refs[count + 1 : 2 * count + 1], refs[2 * count + 1]
    send, recv = refs[2 * count + 2 :]
    me = Place(members)
    me.greet(("core", "y"), False)
    sems = Sems(send, recv)
    rows = ins[0].shape[0]
    half = rows // 2
    first = []
    for src, dst in zip(ins, outs):
        take = pl.ds(pl.multiple_of(me.core * half, 16), half)
        put = pl.ds(pl.multiple_of(me.fsdp * rows + me.core * half, 16), half)
        first.append(sems.copy(src.at[take], dst.at[put], me.partner("y")))
    gain = sems.copy(gain_in, gain_out.at[me.fsdp], me.partner("y"))
    gain_out[me.fsdp] = gain_in[...]
    for src, dst in zip(ins, outs):
        dst[pl.ds(pl.multiple_of(me.fsdp * rows, 16), rows)] = src[...]
    second = []
    for copy, dst in zip(first, outs):
        copy.wait_recv()
        put = pl.ds(pl.multiple_of((1 - me.fsdp) * rows + me.core * half, 16), half)
        second.append(sems.copy(dst.at[put], dst.at[put], me.partner("core")))
    for copy in second:
        copy.wait()
    for copy in first:
        copy.wait_send()
    gain.wait()


def gather_weights(members, weights, gains):
    count = len(weights)
    return pl.pallas_call(
        functools.partial(weights_kernel, members, count),
        out_shape=[jax.ShapeDtypeStruct((2 * w.shape[0], w.shape[1]), w.dtype) for w in weights]
        + [jax.ShapeDtypeStruct((2,) + gains.shape, gains.dtype)],
        in_specs=[VMEM] * (count + 1),
        out_specs=[VMEM] * (count + 1),
        scratch_shapes=[pltpu.SemaphoreType.DMA((2 * count + 1,))] * 2,
        compiler_params=params(0),
    )(*weights, gains)


def keys_kernel(members, kv_ref, grad_ref, out_ref, other_ref, send, recv):
    me = Place(members)
    me.greet(("core", "x", "y"), True)
    sems = Sems(send, recv)
    mine = out_ref.at[me.core, me.x, me.far]
    far = [sems.copy(kv_ref, mine, me.far_device(step)) for step in range(1, members)]
    own = sems.copy(kv_ref, mine, me.partner("x"))
    swap = sems.copy(grad_ref, other_ref, me.partner("y"))
    out_ref[me.core, me.x, me.far] = kv_ref[...]
    along = []
    for step in range(1, members):
        far[step - 1].wait_recv()
        got = out_ref.at[me.core, me.x, me.far_member(members - step)]
        along.append(sems.copy(got, got, me.partner("x")))
    own.wait_recv()
    for copy in along:
        copy.wait_recv()
    block = out_ref.at[me.core]
    last = sems.copy(block, block, me.partner("core"))
    last.wait()
    swap.wait()
    own.wait_send()
    for copy in far + along:
        copy.wait_send()


def gather_keys(members, kv, grad):
    count = 2 * (members - 1) + 3
    return pl.pallas_call(
        functools.partial(keys_kernel, members),
        out_shape=[
            jax.ShapeDtypeStruct((2, 2, members) + kv.shape, kv.dtype),
            jax.ShapeDtypeStruct(grad.shape, grad.dtype),
        ],
        in_specs=[VMEM] * 2,
        out_specs=[VMEM] * 2,
        scratch_shapes=[pltpu.SemaphoreType.DMA((count,))] * 2,
        compiler_params=params(1),
    )(kv, grad)


def swap_kernel(members, count, *refs):
    ins, outs = refs[:count], refs[count : 2 * count]
    send, recv = refs[2 * count :]
    me = Place(members)
    me.greet(("y",), False)
    sems = Sems(send, recv)
    copies = [sems.copy(src, dst, me.partner("y")) for src, dst in zip(ins, outs)]
    for copy in copies:
        copy.wait()


def swap_rows(members, collective_id, *arrays):
    count = len(arrays)
    return pl.pallas_call(
        functools.partial(swap_kernel, members, count),
        out_shape=[jax.ShapeDtypeStruct(a.shape, a.dtype) for a in arrays],
        in_specs=[VMEM] * count,
        out_specs=[VMEM] * count,
        scratch_shapes=[pltpu.SemaphoreType.DMA((count,))] * 2,
        compiler_params=params(collective_id),
    )(*arrays)


def add(a, b):
    return (a.astype(F32) + b.astype(F32)).astype(BF16)


def reduce_kernel(members, flows, has_small, *refs):
    refs = list(refs)
    ins = [refs.pop(0) for _ in flows]
    small_in = refs.pop(0) if has_small else None
    outs = [refs.pop(0) for _ in flows]
    small_out = refs.pop(0) if has_small else None
    gots = [[refs.pop(0) for _ in axes] for axes, _ in flows]
    far_gots = [refs.pop(0) for _ in flows]
    axes_all = []
    for axes, _ in flows:
        axes_all += [axis for axis in axes if axis not in axes_all]
    if has_small:
        small_acc = refs.pop(0)
        small_got = refs.pop(0)
        small_far = refs.pop(0)
    send, recv = refs
    me = Place(members)
    me.greet(tuple(axes_all), True)
    sems = Sems(send, recv)
    sent = []

    def go(src, dst, device):
        copy = sems.copy(src, dst, device)
        sent.append(copy)
        return copy

    flying = []
    for f, (axes, _) in enumerate(flows):
        flying.append(
            go(ins[f].at[1 - me.own(axes[0])], gots[f][0], me.partner(axes[0]))
        )
    depth = max(len(axes) for axes, _ in flows)
    far_flying = [None] * len(flows)
    small = None
    if has_small:
        small_acc[0] = small_in[...]
        small = go(small_acc.at[0], small_got.at[0], me.partner(axes_all[0]))
    for level in range(depth):
        for f, (axes, _) in enumerate(flows):
            if level >= len(axes):
                continue
            flying[f].wait_recv()
            source = ins[f] if level == 0 else gots[f][level - 1]
            held = source.at[me.own(axes[level])]
            got = total = gots[f][level]
            if level + 1 < len(axes):
                away = 1 - me.own(axes[level + 1])
                keep = me.own(axes[level + 1])
                total[away] = add(held[away], got[away])
                flying[f] = go(
                    total.at[away], gots[f][level + 1], me.partner(axes[level + 1])
                )
                total[keep] = add(held[keep], got[keep])
            else:
                far_flying[f] = []
                for step in range(1, members):
                    to = me.far_member(step)
                    total[to] = add(held[to], got[to])
                    far_flying[f].append(
                        go(total.at[to], far_gots[f].at[step - 1], me.far_device(step))
                    )
                total[me.far] = add(held[me.far], got[me.far])
        if has_small:
            small.wait_recv()
            small_acc[level + 1] = small_acc[level] + small_got[level]
            if level + 1 < depth:
                small = go(
                    small_acc.at[level + 1],
                    small_got.at[level + 1],
                    me.partner(axes_all[level + 1]),
                )
            else:
                small = [
                    go(small_acc.at[level + 1], small_far.at[step - 1], me.far_device(step))
                    for step in range(1, members)
                ]
    back = [None] * len(flows)
    for f, (axes, gather) in enumerate(flows):
        whole = gots[f][-1][me.far].astype(F32)
        for step in range(1, members):
            far_flying[f][step - 1].wait_recv()
            whole = whole + far_gots[f][step - 1].astype(F32)
        if not gather:
            outs[f][...] = whole
            continue
        outs[f][me.core, me.x, me.far] = whole.astype(BF16)
        mine = outs[f].at[me.core, me.x, me.far]
        back[f] = [go(mine, mine, me.far_device(step)) for step in range(1, members)]
    if has_small:
        whole = small_acc[depth]
        for step in range(1, members):
            small[step - 1].wait_recv()
            whole = whole + small_far[step - 1]
        small_out[...] = whole
    for axis in ("x", "core"):
        for f, (axes, gather) in enumerate(flows):
            if gather:
                for copy in back[f]:
                    copy.wait_recv()
                block = outs[f].at[me.core, me.x] if axis == "x" else outs[f].at[me.core]
                back[f] = [go(block, block, me.partner(axis))]
    for f, (axes, gather) in enumerate(flows):
        if gather:
            back[f][0].wait_recv()
    for copy in sent:
        copy.wait_send()


def reduce_chunks(members, collective_id, flows, arrays, small=None):
    flows = tuple((tuple(axes), gather) for axes, gather in flows)
    outs, gots, fars, count = [], [], [], 0
    for (axes, gather), array in zip(flows, arrays):
        chunk = array.shape[len(axes) + 1 :]
        if gather:
            outs.append(jax.ShapeDtypeStruct((2, 2, members) + chunk, array.dtype))
        else:
            outs.append(jax.ShapeDtypeStruct(chunk, F32))
        for level in range(len(axes)):
            gots.append(pltpu.VMEM(array.shape[level + 1 :], array.dtype))
        fars.append(pltpu.VMEM((members - 1,) + chunk, array.dtype))
        count += len(axes) + members - 1 + (members + 1 if gather else 0)
    depth = max(len(axes) for axes, _ in flows)
    scratch = gots + fars
    operands = list(arrays)
    if small is not None:
        outs.append(jax.ShapeDtypeStruct(small.shape, small.dtype))
        scratch += [
            pltpu.VMEM((depth + 1,) + small.shape, small.dtype),
            pltpu.VMEM((depth,) + small.shape, small.dtype),
            pltpu.VMEM((members - 1,) + small.shape, small.dtype),
        ]
        operands.append(small)
        count += depth + members - 1
    return pl.pallas_call(
        functools.partial(reduce_kernel, members, flows, small is not None),
        out_shape=outs,
        in_specs=[VMEM] * len(operands),
        out_specs=[VMEM] * len(outs),
        scratch_shapes=scratch + [pltpu.SemaphoreType.DMA((count,))] * 2,
        compiler_params=params(collective_id),
    )(*operands)


def lane_mask(base, head):
    lane = lax.broadcasted_iota(jnp.int32, (1, 2 * KV_WIDTH), 1)
    low = base + head * HEAD_SIZE
    return jnp.where((lane >= low) & (lane < low + HEAD_SIZE), 1.0, 0.0).astype(F32)


def spread(ref, part, base):
    rows = []
    for group in range(GROUP):
        value = ref[part, group].astype(F32)
        for head in range(KEY_VALUE_HEADS):
            rows.append(value * lane_mask(base, head))
    return jnp.concatenate(rows, axis=0)


def fold(value, base, out_ref, part, block):
    for group in range(GROUP):
        total = None
        for head in range(KEY_VALUE_HEADS):
            low = (group * KEY_VALUE_HEADS + head) * block
            piece = value[low : low + block] * lane_mask(base, head)
            total = piece if total is None else total + piece
        out_ref[part, group] = total


def key_window(kv_ref, slot_ref, half, seq, window):
    return jnp.concatenate(
        [
            kv_ref[slot_ref[half * window + j], seq * 2 + slot_ref[(2 + half) * window + j]]
            for j in range(window)
        ],
        axis=0,
    )


def nt(a, b):
    return lax.dot_general(a, b, (((1,), (1,)), ((), ())), preferred_element_type=F32)


def tn(a, b):
    return lax.dot_general(a, b, (((0,), (0,)), ((), ())), preferred_element_type=F32)


def attend_kernel(window, block, slot_ref, q_ref, kv_ref, bias_ref, out_ref, lse_ref):
    for seq in range(2):
        for half in range(2):
            part = seq * 2 + half
            keys = key_window(kv_ref, slot_ref, half, seq, window)
            query = spread(q_ref, part, 0).astype(BF16)
            bias = jnp.concatenate([bias_ref[part]] * QUERY_HEADS, axis=0)
            scores = nt(query, keys) * SCALE + bias
            top = jnp.max(scores, axis=-1, keepdims=True)
            weights = jnp.exp(scores - top)
            total = jnp.sum(weights, axis=-1, keepdims=True)
            probs = (weights / total).astype(BF16)
            mixed = jnp.dot(probs, keys, preferred_element_type=F32)
            fold(mixed, KV_WIDTH, out_ref, part, block)
            lse_ref[part] = top + jnp.log(total)


def attend(slots, query, kv, bias, window, block):
    return pl.pallas_call(
        functools.partial(attend_kernel, window, block),
        out_shape=[
            jax.ShapeDtypeStruct(query.shape, F32),
            jax.ShapeDtypeStruct((4, QUERY_HEADS * block, 1), F32),
        ],
        in_specs=[SMEM] + [VMEM] * 3,
        out_specs=[VMEM] * 2,
        compiler_params=pltpu.CompilerParams(vmem_limit_bytes=60 * 2**20),
    )(slots, query, kv, bias)


def attend_back_kernel(
    window, block, slot_ref, q_ref, kv_ref, bias_ref, grad_ref, o_ref, lse_ref, dq_ref, dkv_ref
):
    dkv_ref[...] = jnp.zeros_like(dkv_ref)
    for seq in range(2):
        for half in range(2):
            part = seq * 2 + half
            keys = key_window(kv_ref, slot_ref, half, seq, window)
            query = spread(q_ref, part, 0).astype(BF16)
            bias = jnp.concatenate([bias_ref[part]] * QUERY_HEADS, axis=0)
            probs = jnp.exp(nt(query, keys) * SCALE + bias - lse_ref[part])
            grad32 = spread(grad_ref, part, KV_WIDTH)
            mixed = spread(o_ref, part, KV_WIDTH)
            delta = jnp.sum(grad32 * mixed, axis=-1, keepdims=True)
            grad = grad32.astype(BF16)
            score_grad = (probs * (nt(grad, keys) - delta)).astype(BF16)
            fold(
                jnp.dot(score_grad, keys, preferred_element_type=F32) * SCALE,
                0,
                dq_ref,
                part,
                block,
            )
            back = tn(score_grad, query) * SCALE + tn(probs.astype(BF16), grad)
            for j in range(window):
                at = slot_ref[half * window + j]
                row = seq * 2 + slot_ref[(2 + half) * window + j]
                dkv_ref[at, row] = add(dkv_ref[at, row], back[j * block : (j + 1) * block])


def attend_back(slots, query, kv, bias, grad, mixed, lse, window, block):
    return pl.pallas_call(
        functools.partial(attend_back_kernel, window, block),
        out_shape=[
            jax.ShapeDtypeStruct(query.shape, F32),
            jax.ShapeDtypeStruct(kv.shape, kv.dtype),
        ],
        in_specs=[SMEM] + [VMEM] * 6,
        out_specs=[VMEM] * 2,
        compiler_params=pltpu.CompilerParams(vmem_limit_bytes=60 * 2**20),
    )(slots, query, kv, bias, grad, mixed, lse)


def rope_tables(token_positions):
    half = HEAD_SIZE // 2
    freq = theta_base ** (-jnp.arange(half, dtype=jnp.float32) * 2.0 / HEAD_SIZE)
    angles = token_positions.astype(jnp.float32)[:, None] * freq[None, :]
    cosine_table = jnp.concatenate([jnp.cos(angles), jnp.cos(angles)], axis=-1)
    sine_table = jnp.concatenate([jnp.sin(angles), jnp.sin(angles)], axis=-1)
    return (cosine_table[:, None, :], sine_table[:, None, :])


def rotary_apply(value_rows, cosine_table, sine_table):
    half = value_rows.shape[-1] // 2
    turned = jnp.concatenate([-value_rows[..., half:], value_rows[..., :half]], axis=-1)
    return value_rows * cosine_table + turned * sine_table


def rotary_inverse(grads, cosine_table, sine_table):
    half = grads.shape[-1] // 2
    scaled = grads * sine_table
    turned = jnp.concatenate([scaled[..., half:], -scaled[..., :half]], axis=-1)
    return grads * cosine_table + turned


def normalize(value_rows):
    inverse = lax.rsqrt(jnp.mean(value_rows * value_rows, axis=-1, keepdims=True) + epsilon)
    return (inverse, value_rows * inverse)


def rms_back(grads, inverse, normed):
    return inverse * (grads - normed * jnp.mean(grads * normed, axis=-1, keepdims=True))


def outer_sum(left, right):
    flat_left = left.reshape(-1, left.shape[-1])
    flat_right = right.reshape(-1, right.shape[-1])
    return lax.dot_general(
        flat_left, flat_right, (((0,), (0,)), ((), ())), preferred_element_type=jnp.float32
    )


def back_dot(grads, weight):
    return lax.dot_general(
        grads, weight, (((grads.ndim - 1,), (1,)), ((), ())), preferred_element_type=jnp.float32
    )


def to_groups(rows, block):
    split = rows.reshape(-1, block, KEY_VALUE_HEADS, GROUP, HEAD_SIZE)
    return jnp.transpose(split, (0, 3, 1, 2, 4)).reshape(-1, GROUP, block, KV_WIDTH)


def from_groups(parts, block):
    split = parts.reshape(-1, GROUP, block, KEY_VALUE_HEADS, HEAD_SIZE)
    return jnp.transpose(split, (0, 2, 3, 1, 4)).reshape(2, 2 * block, QUERY_HEADS * HEAD_SIZE)


def chunks(rows, members):
    count = 4 * members
    each = -(-rows.shape[0] // (count * 16)) * 16
    padded = jnp.pad(rows, ((0, count * each - rows.shape[0]), (0, 0)))
    return padded.reshape(2, 2, members, each, rows.shape[1])


def unchunk(array, rows):
    return array.reshape(-1, array.shape[-1])[:rows]


def body(
    tokens,
    query_matrix,
    key_projection,
    value_projection,
    output_matrix,
    attn_gain,
    mlp_gain,
    gate_matrix,
    up_matrix,
    down_matrix,
    pair_table,
    doc_ids,
    out_grad,
):
    sequence_group, token_per_shard, width = tokens.shape
    pairs = lax.axis_size("ctx")
    members = pairs // 4
    block = token_per_shard // 2
    length = token_per_shard * pairs
    blocks = 2 * pairs
    window = length // 8 // block + 1
    rows = sequence_group * token_per_shard
    me_f = lax.axis_index("fsdp")

    gains = jnp.pad(
        jnp.stack([attn_gain, mlp_gain]).astype(F32), ((0, 6), (0, 0))
    )
    query_full, key_full, value_full, output_full, gains_full = gather_weights(
        members, (query_matrix, key_projection, value_projection, output_matrix), gains
    )
    attn_gain_f = gains_full[:, 0].reshape(width)
    mlp_gain_f = gains_full[:, 1].reshape(width)

    table_row = lax.dynamic_index_in_dim(pair_table, lax.axis_index("ctx"), 0, keepdims=False)
    local = jnp.arange(token_per_shard, dtype=jnp.int32)
    own_pos = jnp.where(local < block, table_row[0], table_row[1]) * block + local % block
    cosine_table, sine_table = rope_tables(own_pos)

    block_ids = jnp.arange(blocks, dtype=jnp.int32)
    where_dealt = jnp.sum(
        block_ids[None, :]
        * (pair_table.reshape(-1)[None, :] == block_ids[:, None]).astype(jnp.int32),
        axis=1,
    )
    span = window * block
    padded_docs = jnp.pad(doc_ids, ((0, 0), (span - block, 0)), constant_values=-1)
    padded_slots = jnp.pad(where_dealt, (window - 1, 0))
    slot_parts, bias_parts = [], []
    offset = jnp.arange(span, dtype=jnp.int32)
    for half in range(2):
        at = table_row[half]
        slot_parts.append(lax.dynamic_slice_in_dim(padded_slots, at, window, 0))
        key_doc = lax.dynamic_slice_in_dim(padded_docs, at * block, span, 1)
        query_doc = key_doc[:, span - block :]
        causal = offset[None, :] <= offset[:block, None] + (span - block)
        allowed = causal[None] & (key_doc[:, None, :] == query_doc[:, :, None])
        bias_parts.append(jnp.where(allowed, 0.0, masked_logits))
    slots = jnp.concatenate(slot_parts)
    owner, which = slots // 2, slots % 2
    lies = (owner % 2) * (2 * members) + (owner // 2 % 2) * members + owner // 4
    slots = jnp.concatenate([lies, which]).astype(jnp.int32)
    bias = jnp.stack(bias_parts, axis=1).reshape(2 * sequence_group, block, span).astype(F32)

    inputs = tokens.astype(F32)
    inv_one, normed_one = normalize(inputs)
    hidden_one = (normed_one * attn_gain_f).astype(BF16)
    query_lin = jnp.dot(hidden_one, query_full, preferred_element_type=F32).reshape(
        sequence_group, token_per_shard, QUERY_HEADS, HEAD_SIZE
    )
    key_linear = jnp.dot(hidden_one, key_full, preferred_element_type=F32).reshape(
        sequence_group, token_per_shard, KEY_VALUE_HEADS, HEAD_SIZE
    )
    value_rows = jnp.dot(hidden_one, value_full, preferred_element_type=F32).astype(BF16)
    query_rows = rotary_apply(query_lin, cosine_table, sine_table).astype(BF16)
    key_rows = (
        rotary_apply(key_linear, cosine_table, sine_table)
        .astype(BF16)
        .reshape(sequence_group, token_per_shard, KV_WIDTH)
    )
    own_kv = jnp.concatenate([key_rows, value_rows], axis=-1).reshape(
        2 * sequence_group, block, 2 * KV_WIDTH
    )
    flat_grad = out_grad.reshape(rows, width)
    kv_all, other_grad = gather_keys(members, own_kv, flat_grad)
    kv_all = kv_all.reshape(pairs, 2 * sequence_group, block, 2 * KV_WIDTH)

    query_parts = jnp.pad(to_groups(query_rows, block), ((0, 0), (0, 0), (0, 0), (0, KV_WIDTH)))
    mixed_parts, lse = attend(slots, query_parts, kv_all, bias, window, block)
    attn_in = from_groups(mixed_parts[..., KV_WIDTH:].astype(BF16), block)

    mixed_heads = inputs + jnp.dot(attn_in, output_full, preferred_element_type=F32)
    inv_two, normed_two = normalize(mixed_heads)
    hidden_two = (normed_two * mlp_gain_f).astype(BF16).reshape(rows, width)

    (other_hidden,) = swap_rows(members, 2, hidden_two)
    hid = jnp.concatenate([hidden_two, other_hidden])
    grads = jnp.concatenate([flat_grad, other_grad])
    gate = jnp.dot(hid, gate_matrix, preferred_element_type=F32)
    upper = jnp.dot(hid, up_matrix, preferred_element_type=F32)
    sigma = jax.nn.sigmoid(gate)
    activated = (gate * sigma * upper).astype(BF16)
    act_grad = back_dot(grads, down_matrix)
    up_grad_r = (act_grad * gate * sigma).astype(BF16)
    gate_grad_r = (act_grad * upper * sigma * (1.0 + gate * (1.0 - sigma))).astype(BF16)
    branch = jnp.dot(activated, down_matrix, preferred_element_type=F32)
    hidden_grad = back_dot(gate_grad_r, gate_matrix) + back_dot(up_grad_r, up_matrix)
    other_branch, other_hidden_grad = swap_rows(
        members, 3, branch[rows:].astype(BF16), hidden_grad[rows:].astype(BF16)
    )
    shape = (sequence_group, token_per_shard, width)
    branch_out = (branch[:rows] + other_branch.astype(F32)).reshape(shape)
    hidden_two_grad = (hidden_grad[:rows] + other_hidden_grad.astype(F32)).reshape(shape)
    units = gate_matrix.shape[1]
    gate_wgrad = chunks(outer_sum(gate_grad_r, hid).astype(BF16), members)
    up_wgrad = chunks(outer_sum(up_grad_r, hid).astype(BF16), members)
    down_wgrad = chunks(outer_sum(activated, grads).astype(BF16), members)

    block_out = (mixed_heads + branch_out).astype(BF16)
    mlp_gain_wgrad = jnp.sum(hidden_two_grad * normed_two, axis=(0, 1))
    mixed_grad = out_grad.astype(F32) + rms_back(
        hidden_two_grad * mlp_gain_f, inv_two, normed_two
    )
    branch_grad = mixed_grad.astype(BF16)
    attn_grad = back_dot(branch_grad, output_full).astype(BF16)
    grad_parts = jnp.pad(to_groups(attn_grad, block), ((0, 0), (0, 0), (0, 0), (KV_WIDTH, 0)))
    query_back, kv_back = attend_back(
        slots, query_parts, kv_all, bias, grad_parts, mixed_parts, lse, window, block
    )
    kv_sum, gate_total, up_total, down_total = reduce_chunks(
        members,
        4,
        ((("core", "x"), False),) + ((("core", "x"), True),) * 3,
        (
            kv_back.reshape(2, 2, members, rows, 2 * KV_WIDTH),
            gate_wgrad,
            up_wgrad,
            down_wgrad,
        ),
    )
    query_grad_r = (
        rotary_inverse(
            from_groups(query_back[..., :KV_WIDTH], block).reshape(
                sequence_group, token_per_shard, QUERY_HEADS, HEAD_SIZE
            ),
            cosine_table,
            sine_table,
        )
        .reshape(sequence_group, token_per_shard, QUERY_HEADS * HEAD_SIZE)
        .astype(BF16)
    )
    kv_sum = kv_sum.reshape(sequence_group, token_per_shard, 2 * KV_WIDTH)
    key_grad_r = (
        rotary_inverse(
            kv_sum[..., :KV_WIDTH].reshape(
                sequence_group, token_per_shard, KEY_VALUE_HEADS, HEAD_SIZE
            ),
            cosine_table,
            sine_table,
        )
        .reshape(sequence_group, token_per_shard, KV_WIDTH)
        .astype(BF16)
    )
    value_grad_r = kv_sum[..., KV_WIDTH:].astype(BF16)
    hidden_one_grad = (
        back_dot(query_grad_r, query_full)
        + back_dot(key_grad_r, key_full)
        + back_dot(value_grad_r, value_full)
    )
    attn_gain_wgrad = jnp.sum(hidden_one_grad * normed_one, axis=(0, 1))
    input_grad = mixed_grad + rms_back(hidden_one_grad * attn_gain_f, inv_one, normed_one)

    part = query_matrix.shape[0]
    qkv = jnp.concatenate([query_grad_r, key_grad_r, value_grad_r], axis=-1)
    qkv_wgrad = outer_sum(qkv, hidden_one).astype(BF16)
    output_wgrad = outer_sum(branch_grad, attn_in).astype(BF16)
    both = jnp.concatenate([qkv_wgrad, output_wgrad])
    count = both.shape[0] // 2
    sides = []
    for side in range(2):
        piece = both[:, side * part : (side + 1) * part]
        sides.append(chunks(jnp.concatenate([piece[:count], piece[count:]], axis=1), members))
    small = jnp.pad(jnp.stack([attn_gain_wgrad, mlp_gain_wgrad]), ((0, 6), (0, 0)))
    attn_total, small_total = reduce_chunks(
        members,
        5,
        ((("core", "y", "x"), True),),
        (jnp.stack(sides, axis=1),),
        small,
    )
    flat = unchunk(attn_total, count)
    columns = jnp.concatenate([flat[:, :part], flat[:, part:]]).astype(F32)
    whole = columns.T
    kept = lax.dynamic_slice_in_dim(small_total, me_f * part, part, 1)
    heads = QUERY_HEADS * HEAD_SIZE
    return (
        block_out,
        input_grad,
        whole[:, :heads],
        whole[:, heads : heads + KV_WIDTH],
        whole[:, heads + KV_WIDTH : heads + 2 * KV_WIDTH],
        whole[:, heads + 2 * KV_WIDTH :],
        kept[0],
        kept[1],
        unchunk(gate_total, units).T.astype(F32),
        unchunk(up_total, units).T.astype(F32),
        unchunk(down_total, units).astype(F32),
    )


def solution(mesh):
    return jax.shard_map(
        body,
        mesh=mesh,
        in_specs=(
            P("fsdp", "ctx", None),
            P("fsdp", None),
            P("fsdp", None),
            P("fsdp", None),
            P("fsdp", None),
            P("fsdp"),
            P("fsdp"),
            P(None, "fsdp"),
            P(None, "fsdp"),
            P("fsdp", None),
            P(),
            P("fsdp", None),
            P("fsdp", "ctx", None),
        ),
        out_specs=(
            P("fsdp", "ctx", None),
            P("fsdp", "ctx", None),
            P("fsdp", None),
            P("fsdp", None),
            P("fsdp", None),
            P("fsdp", None),
            P("fsdp"),
            P("fsdp"),
            P(None, "fsdp"),
            P(None, "fsdp"),
            P("fsdp", None),
        ),
        check_vma=False,
    )
```

```python
import functools
import math

import jax
import jax.numpy as jnp
from jax import lax
from jax.experimental import pallas as pl
from jax.experimental.pallas import tpu as pltpu
from jax.sharding import PartitionSpec as P

QUERY_HEADS = 9
KEY_VALUE_HEADS = 3
HEAD_SIZE = 64
GROUP = QUERY_HEADS // KEY_VALUE_HEADS
KV_WIDTH = KEY_VALUE_HEADS * HEAD_SIZE
SCALE = 1.0 / math.sqrt(HEAD_SIZE)

epsilon = 1e-05
theta_base = 10000.0
masked_logits = -1e30

VMEM = pl.BlockSpec(memory_space=pltpu.VMEM)
SMEM = pl.BlockSpec(memory_space=pltpu.SMEM)
MESH = pl.DeviceIdType.MESH
F32 = jnp.float32
BF16 = jnp.bfloat16


class Place:
    def __init__(self, members):
        self.members = members
        self.ctx = lax.axis_index("ctx")
        self.fsdp = lax.axis_index("fsdp")
        self.core = self.ctx % 2
        self.x = (self.ctx // 2) % 2
        self.far = self.ctx // 4

    def own(self, axis):
        return {"core": self.core, "x": self.x, "y": self.fsdp}[axis]

    def partner(self, axis):
        if axis == "core":
            return (self.ctx + 1 - 2 * self.core, self.fsdp)
        if axis == "x":
            return (self.ctx + 2 - 4 * self.x, self.fsdp)
        return (self.ctx, 1 - self.fsdp)

    def far_member(self, step):
        return (self.far + step) % self.members

    def far_device(self, step):
        return (self.far_member(step) * 4 + self.ctx % 4, self.fsdp)

    def greet(self, axes, far):
        barrier = pltpu.get_barrier_semaphore()
        for axis in axes:
            pl.semaphore_signal(barrier, inc=1, device_id=self.partner(axis), device_id_type=MESH)
        count = len(axes)
        if far:
            for step in range(1, self.members):
                pl.semaphore_signal(
                    barrier, inc=1, device_id=self.far_device(step), device_id_type=MESH
                )
            count += self.members - 1
        pl.semaphore_wait(barrier, count)


class Sems:
    def __init__(self, send, recv):
        self.send, self.recv, self.at = send, recv, 0

    def copy(self, src, dst, device):
        at = self.at
        self.at += 1
        made = pltpu.make_async_remote_copy(
            src_ref=src,
            dst_ref=dst,
            send_sem=self.send.at[at],
            recv_sem=self.recv.at[at],
            device_id=device,
            device_id_type=MESH,
        )
        made.start()
        return made


def params(collective_id):
    return pltpu.CompilerParams(
        collective_id=collective_id, has_side_effects=True, vmem_limit_bytes=60 * 2**20
    )


def weights_kernel(members, count, *refs):
    ins, gain_in = refs[:count], refs[count]
    outs, gain_out = refs[count + 1 : 2 * count + 1], refs[2 * count + 1]
    send, recv = refs[2 * count + 2 :]
    me = Place(members)
    me.greet(("core", "y"), False)
    sems = Sems(send, recv)
    rows = ins[0].shape[0]
    half = rows // 2
    first = []
    for src, dst in zip(ins, outs):
        take = pl.ds(pl.multiple_of(me.core * half, 16), half)
        put = pl.ds(pl.multiple_of(me.fsdp * rows + me.core * half, 16), half)
        first.append(sems.copy(src.at[take], dst.at[put], me.partner("y")))
    gain = sems.copy(gain_in, gain_out.at[me.fsdp], me.partner("y"))
    gain_out[me.fsdp] = gain_in[...]
    for src, dst in zip(ins, outs):
        dst[pl.ds(pl.multiple_of(me.fsdp * rows, 16), rows)] = src[...]
    second = []
    for copy, dst in zip(first, outs):
        copy.wait_recv()
        put = pl.ds(pl.multiple_of((1 - me.fsdp) * rows + me.core * half, 16), half)
        second.append(sems.copy(dst.at[put], dst.at[put], me.partner("core")))
    for copy in second:
        copy.wait()
    for copy in first:
        copy.wait_send()
    gain.wait()


def gather_weights(members, weights, gains):
    count = len(weights)
    return pl.pallas_call(
        functools.partial(weights_kernel, members, count),
        out_shape=[jax.ShapeDtypeStruct((2 * w.shape[0], w.shape[1]), w.dtype) for w in weights]
        + [jax.ShapeDtypeStruct((2,) + gains.shape, gains.dtype)],
        in_specs=[VMEM] * (count + 1),
        out_specs=[VMEM] * (count + 1),
        scratch_shapes=[pltpu.SemaphoreType.DMA((2 * count + 1,))] * 2,
        compiler_params=params(0),
    )(*weights, gains)


def keys_kernel(
    members, kv_ref, grad_ref, w_ref, out_ref, other_ref, full_ref, send, recv
):
    me = Place(members)
    me.greet(("core", "x", "y"), True)
    sems = Sems(send, recv)
    rows = w_ref.shape[0]
    half = rows // 2
    mine = out_ref.at[me.core, me.x, me.far]
    far = [sems.copy(kv_ref, mine, me.far_device(step)) for step in range(1, members)]
    own = sems.copy(kv_ref, mine, me.partner("x"))
    put = pl.ds(pl.multiple_of(me.fsdp * rows + me.core * half, 16), half)
    weight = sems.copy(
        w_ref.at[pl.ds(pl.multiple_of(me.core * half, 16), half)],
        full_ref.at[put],
        me.partner("y"),
    )
    swap = sems.copy(grad_ref, other_ref, me.partner("y"))
    out_ref[me.core, me.x, me.far] = kv_ref[...]
    full_ref[pl.ds(pl.multiple_of(me.fsdp * rows, 16), rows)] = w_ref[...]
    along = []
    for step in range(1, members):
        far[step - 1].wait_recv()
        got = out_ref.at[me.core, me.x, me.far_member(members - step)]
        along.append(sems.copy(got, got, me.partner("x")))
    weight.wait_recv()
    put = pl.ds(pl.multiple_of((1 - me.fsdp) * rows + me.core * half, 16), half)
    across = sems.copy(full_ref.at[put], full_ref.at[put], me.partner("core"))
    block = out_ref.at[me.core, me.x]
    near = sems.copy(block, block, me.partner("core"))
    own.wait_recv()
    for copy in along:
        copy.wait_recv()
    block = out_ref.at[me.core, 1 - me.x]
    last = sems.copy(block, block, me.partner("core"))
    for copy in (near, last, across, swap):
        copy.wait()
    for copy in far + along + [own, weight]:
        copy.wait_send()


def gather_keys(members, kv, grad, weight):
    count = 2 * (members - 1) + 6
    return pl.pallas_call(
        functools.partial(keys_kernel, members),
        out_shape=[
            jax.ShapeDtypeStruct((2, 2, members) + kv.shape, kv.dtype),
            jax.ShapeDtypeStruct(grad.shape, grad.dtype),
            jax.ShapeDtypeStruct((2 * weight.shape[0], weight.shape[1]), weight.dtype),
        ],
        in_specs=[VMEM] * 3,
        out_specs=[VMEM] * 3,
        scratch_shapes=[pltpu.SemaphoreType.DMA((count,))] * 2,
        compiler_params=params(1),
    )(kv, grad, weight)


def swap_kernel(members, count, *refs):
    ins, outs = refs[:count], refs[count : 2 * count]
    send, recv = refs[2 * count :]
    me = Place(members)
    me.greet(("y",), False)
    sems = Sems(send, recv)
    copies = [sems.copy(src, dst, me.partner("y")) for src, dst in zip(ins, outs)]
    for copy in copies:
        copy.wait()


def swap_rows(members, collective_id, *arrays):
    count = len(arrays)
    return pl.pallas_call(
        functools.partial(swap_kernel, members, count),
        out_shape=[jax.ShapeDtypeStruct(a.shape, a.dtype) for a in arrays],
        in_specs=[VMEM] * count,
        out_specs=[VMEM] * count,
        scratch_shapes=[pltpu.SemaphoreType.DMA((count,))] * 2,
        compiler_params=params(collective_id),
    )(*arrays)


def add(a, b):
    return (a.astype(F32) + b.astype(F32)).astype(BF16)


def reduce_kernel(members, kinds, flows, has_small, *refs):
    refs = list(refs)
    ins = [refs.pop(0) for _ in kinds]
    small_in = refs.pop(0) if has_small else None
    outs = [refs.pop(0) for _ in kinds]
    small_out = refs.pop(0) if has_small else None
    gots = [[refs.pop(0) for _ in kinds[array][0]] for array, _, _ in flows]
    far_gots = [refs.pop(0) for _ in flows]
    axes_all = []
    for axes, _ in kinds:
        axes_all += [axis for axis in axes if axis not in axes_all]
    if has_small:
        small_acc, small_got, small_far = [refs.pop(0) for _ in range(3)]
    send, recv = refs
    me = Place(members)
    me.greet(tuple(axes_all), True)
    sems = Sems(send, recv)
    sent = []

    def go(src, dst, device):
        copy = sems.copy(src, dst, device)
        sent.append(copy)
        return copy

    def steps(f):
        array, low, rows = flows[f]
        axes, gather = kinds[array]
        cut = pl.ds(low, rows)

        def part(index):
            return ins[array].at[(index,) + (slice(None),) * len(axes) + (cut,)]

        flying = go(part(1 - me.own(axes[0])), gots[f][0], me.partner(axes[0]))
        yield
        for level, axis in enumerate(axes):
            flying.wait_recv()
            held = part(me.own(axis)) if level == 0 else gots[f][level - 1].at[me.own(axis)]
            got = gots[f][level]
            if level + 1 < len(axes):
                keep = me.own(axes[level + 1])
                away = 1 - keep
                got[away] = add(held[away], got[away])
                flying = go(got.at[away], gots[f][level + 1], me.partner(axes[level + 1]))
                got[keep] = add(held[keep], got[keep])
            else:
                spread_out = []
                for step in range(1, members):
                    to = me.far_member(step)
                    got[to] = add(held[to], got[to])
                    spread_out.append(
                        go(got.at[to], far_gots[f].at[step - 1], me.far_device(step))
                    )
                got[me.far] = add(held[me.far], got[me.far])
            yield
        whole = gots[f][-1][me.far].astype(F32)
        for step in range(1, members):
            spread_out[step - 1].wait_recv()
            whole = whole + far_gots[f][step - 1].astype(F32)
        if not gather:
            outs[array][cut] = whole
            return
        outs[array][me.core, me.x, me.far, cut] = whole.astype(BF16)
        mine = outs[array].at[me.core, me.x, me.far, cut]
        back = [go(mine, mine, me.far_device(step)) for step in range(1, members)]
        yield
        for copy in back:
            copy.wait_recv()
        block = outs[array].at[me.core, me.x, :, cut]
        flying = go(block, block, me.partner("x"))
        yield
        flying.wait_recv()
        block = outs[array].at[me.core, :, :, cut]
        flying = go(block, block, me.partner("core"))
        yield
        flying.wait_recv()

    def small_steps():
        depth = len(axes_all)
        small_acc[0] = small_in[...]
        for level in range(depth):
            flying = go(small_acc.at[level], small_got.at[level], me.partner(axes_all[level]))
            yield
            flying.wait_recv()
            small_acc[level + 1] = small_acc[level] + small_got[level]
        last = [
            go(small_acc.at[depth], small_far.at[step - 1], me.far_device(step))
            for step in range(1, members)
        ]
        yield
        whole = small_acc[depth]
        for step in range(1, members):
            last[step - 1].wait_recv()
            whole = whole + small_far[step - 1]
        small_out[...] = whole

    line = [steps(f) for f in range(len(flows))]
    starts = [max(0, f - 2) for f in range(len(flows))]
    if has_small:
        line.append(small_steps())
        starts.append(0)
    live, now = set(range(len(line))), 0
    while live:
        for f in sorted(live):
            if now >= starts[f] and next(line[f], True):
                live.discard(f)
        now += 1
    for copy in sent:
        copy.wait_send()


def reduce_chunks(members, collective_id, kinds, arrays, pieces, small=None):
    kinds = tuple((tuple(axes), gather) for axes, gather in kinds)
    outs, gots, fars, flows, count = [], [], [], [], 0
    for at, ((axes, gather), array) in enumerate(zip(kinds, arrays)):
        chunk = array.shape[len(axes) + 1 :]
        if gather:
            outs.append(jax.ShapeDtypeStruct((2, 2, members) + chunk, array.dtype))
        else:
            outs.append(jax.ShapeDtypeStruct(chunk, F32))
        low = 0
        while low < chunk[0]:
            rows = min(pieces, chunk[0] - low)
            flows.append((at, low, rows))
            low += rows
            for level in range(len(axes)):
                lead = array.shape[level + 1 : len(axes) + 1]
                gots.append(pltpu.VMEM(lead + (rows,) + chunk[1:], array.dtype))
            fars.append(pltpu.VMEM((members - 1, rows) + chunk[1:], array.dtype))
            count += len(axes) + members - 1 + (members + 1 if gather else 0)
    scratch = gots + fars
    operands = list(arrays)
    if small is not None:
        depth = max(len(axes) for axes, _ in kinds)
        outs.append(jax.ShapeDtypeStruct(small.shape, small.dtype))
        scratch += [
            pltpu.VMEM((depth + 1,) + small.shape, small.dtype),
            pltpu.VMEM((depth,) + small.shape, small.dtype),
            pltpu.VMEM((members - 1,) + small.shape, small.dtype),
        ]
        operands.append(small)
        count += depth + members - 1
    return pl.pallas_call(
        functools.partial(reduce_kernel, members, kinds, tuple(flows), small is not None),
        out_shape=outs,
        in_specs=[VMEM] * len(operands),
        out_specs=[VMEM] * len(outs),
        scratch_shapes=scratch + [pltpu.SemaphoreType.DMA((count,))] * 2,
        compiler_params=params(collective_id),
    )(*operands)


def lane_mask(base, head):
    lane = lax.broadcasted_iota(jnp.int32, (1, 2 * KV_WIDTH), 1)
    low = base + head * HEAD_SIZE
    return jnp.where((lane >= low) & (lane < low + HEAD_SIZE), 1.0, 0.0).astype(F32)


def spread(ref, part, base):
    rows = []
    for group in range(GROUP):
        value = ref[part, group].astype(F32)
        for head in range(KEY_VALUE_HEADS):
            rows.append(value * lane_mask(base, head))
    return jnp.concatenate(rows, axis=0)


def fold(value, base, out_ref, part, block):
    for group in range(GROUP):
        total = None
        for head in range(KEY_VALUE_HEADS):
            low = (group * KEY_VALUE_HEADS + head) * block
            piece = value[low : low + block] * lane_mask(base, head)
            total = piece if total is None else total + piece
        out_ref[part, group] = total


def key_window(kv_ref, slot_ref, half, seq, window):
    return jnp.concatenate(
        [
            kv_ref[slot_ref[half * window + j], seq * 2 + slot_ref[(2 + half) * window + j]]
            for j in range(window)
        ],
        axis=0,
    )


def nt(a, b):
    return lax.dot_general(a, b, (((1,), (1,)), ((), ())), preferred_element_type=F32)


def tn(a, b):
    return lax.dot_general(a, b, (((0,), (0,)), ((), ())), preferred_element_type=F32)


def attend_kernel(window, block, slot_ref, q_ref, kv_ref, bias_ref, out_ref, lse_ref):
    for seq in range(2):
        for half in range(2):
            part = seq * 2 + half
            keys = key_window(kv_ref, slot_ref, half, seq, window)
            query = spread(q_ref, part, 0).astype(BF16)
            bias = jnp.concatenate([bias_ref[part]] * QUERY_HEADS, axis=0)
            scores = nt(query, keys) * SCALE + bias
            top = jnp.max(scores, axis=-1, keepdims=True)
            weights = jnp.exp(scores - top)
            total = jnp.sum(weights, axis=-1, keepdims=True)
            probs = (weights / total).astype(BF16)
            mixed = jnp.dot(probs, keys, preferred_element_type=F32)
            fold(mixed, KV_WIDTH, out_ref, part, block)
            lse_ref[part] = top + jnp.log(total)


def attend(slots, query, kv, bias, window, block):
    return pl.pallas_call(
        functools.partial(attend_kernel, window, block),
        out_shape=[
            jax.ShapeDtypeStruct(query.shape, F32),
            jax.ShapeDtypeStruct((4, QUERY_HEADS * block, 1), F32),
        ],
        in_specs=[SMEM] + [VMEM] * 3,
        out_specs=[VMEM] * 2,
        compiler_params=pltpu.CompilerParams(vmem_limit_bytes=60 * 2**20),
    )(slots, query, kv, bias)


def attend_back_kernel(
    window, block, slot_ref, q_ref, kv_ref, bias_ref, grad_ref, o_ref, lse_ref, dq_ref, dkv_ref
):
    dkv_ref[...] = jnp.zeros_like(dkv_ref)
    for seq in range(2):
        for half in range(2):
            part = seq * 2 + half
            keys = key_window(kv_ref, slot_ref, half, seq, window)
            query = spread(q_ref, part, 0).astype(BF16)
            bias = jnp.concatenate([bias_ref[part]] * QUERY_HEADS, axis=0)
            probs = jnp.exp(nt(query, keys) * SCALE + bias - lse_ref[part])
            grad32 = spread(grad_ref, part, KV_WIDTH)
            mixed = spread(o_ref, part, KV_WIDTH)
            delta = jnp.sum(grad32 * mixed, axis=-1, keepdims=True)
            grad = grad32.astype(BF16)
            score_grad = (probs * (nt(grad, keys) - delta)).astype(BF16)
            fold(
                jnp.dot(score_grad, keys, preferred_element_type=F32) * SCALE,
                0,
                dq_ref,
                part,
                block,
            )
            back = tn(score_grad, query) * SCALE + tn(probs.astype(BF16), grad)
            for j in range(window):
                at = slot_ref[half * window + j]
                row = seq * 2 + slot_ref[(2 + half) * window + j]
                dkv_ref[at, row] = add(dkv_ref[at, row], back[j * block : (j + 1) * block])


def attend_back(slots, query, kv, bias, grad, mixed, lse, window, block):
    return pl.pallas_call(
        functools.partial(attend_back_kernel, window, block),
        out_shape=[
            jax.ShapeDtypeStruct(query.shape, F32),
            jax.ShapeDtypeStruct(kv.shape, kv.dtype),
        ],
        in_specs=[SMEM] + [VMEM] * 6,
        out_specs=[VMEM] * 2,
        compiler_params=pltpu.CompilerParams(vmem_limit_bytes=60 * 2**20),
    )(slots, query, kv, bias, grad, mixed, lse)


def rope_tables(token_positions):
    half = HEAD_SIZE // 2
    freq = theta_base ** (-jnp.arange(half, dtype=jnp.float32) * 2.0 / HEAD_SIZE)
    angles = token_positions.astype(jnp.float32)[:, None] * freq[None, :]
    cosine_table = jnp.concatenate([jnp.cos(angles), jnp.cos(angles)], axis=-1)
    sine_table = jnp.concatenate([jnp.sin(angles), jnp.sin(angles)], axis=-1)
    return (cosine_table[:, None, :], sine_table[:, None, :])


def rotary_apply(value_rows, cosine_table, sine_table):
    half = value_rows.shape[-1] // 2
    turned = jnp.concatenate([-value_rows[..., half:], value_rows[..., :half]], axis=-1)
    return value_rows * cosine_table + turned * sine_table


def rotary_inverse(grads, cosine_table, sine_table):
    half = grads.shape[-1] // 2
    scaled = grads * sine_table
    turned = jnp.concatenate([scaled[..., half:], -scaled[..., :half]], axis=-1)
    return grads * cosine_table + turned


def normalize(value_rows):
    inverse = lax.rsqrt(jnp.mean(value_rows * value_rows, axis=-1, keepdims=True) + epsilon)
    return (inverse, value_rows * inverse)


def rms_back(grads, inverse, normed):
    return inverse * (grads - normed * jnp.mean(grads * normed, axis=-1, keepdims=True))


def outer_sum(left, right):
    flat_left = left.reshape(-1, left.shape[-1])
    flat_right = right.reshape(-1, right.shape[-1])
    return lax.dot_general(
        flat_left, flat_right, (((0,), (0,)), ((), ())), preferred_element_type=jnp.float32
    )


def back_dot(grads, weight):
    return lax.dot_general(
        grads, weight, (((grads.ndim - 1,), (1,)), ((), ())), preferred_element_type=jnp.float32
    )


def to_groups(rows, block):
    split = rows.reshape(-1, block, KEY_VALUE_HEADS, GROUP, HEAD_SIZE)
    return jnp.transpose(split, (0, 3, 1, 2, 4)).reshape(-1, GROUP, block, KV_WIDTH)


def from_groups(parts, block):
    split = parts.reshape(-1, GROUP, block, KEY_VALUE_HEADS, HEAD_SIZE)
    return jnp.transpose(split, (0, 2, 3, 1, 4)).reshape(2, 2 * block, QUERY_HEADS * HEAD_SIZE)


def chunks(rows, members):
    count = 4 * members
    each = -(-rows.shape[0] // (count * 16)) * 16
    padded = jnp.pad(rows, ((0, count * each - rows.shape[0]), (0, 0)))
    return padded.reshape(2, 2, members, each, rows.shape[1])


def unchunk(array, rows):
    return array.reshape(-1, array.shape[-1])[:rows]


def body(
    tokens,
    query_matrix,
    key_projection,
    value_projection,
    output_matrix,
    attn_gain,
    mlp_gain,
    gate_matrix,
    up_matrix,
    down_matrix,
    pair_table,
    doc_ids,
    out_grad,
):
    sequence_group, token_per_shard, width = tokens.shape
    pairs = lax.axis_size("ctx")
    members = pairs // 4
    block = token_per_shard // 2
    length = token_per_shard * pairs
    blocks = 2 * pairs
    window = length // 8 // block + 1
    rows = sequence_group * token_per_shard
    me_f = lax.axis_index("fsdp")

    gains = jnp.pad(
        jnp.stack([attn_gain, mlp_gain]).astype(F32), ((0, 6), (0, 0))
    )
    query_full, key_full, value_full, gains_full = gather_weights(
        members, (query_matrix, key_projection, value_projection), gains
    )
    attn_gain_f = gains_full[:, 0].reshape(width)
    mlp_gain_f = gains_full[:, 1].reshape(width)

    table_row = lax.dynamic_index_in_dim(pair_table, lax.axis_index("ctx"), 0, keepdims=False)
    local = jnp.arange(token_per_shard, dtype=jnp.int32)
    own_pos = jnp.where(local < block, table_row[0], table_row[1]) * block + local % block
    cosine_table, sine_table = rope_tables(own_pos)

    block_ids = jnp.arange(blocks, dtype=jnp.int32)
    where_dealt = jnp.sum(
        block_ids[None, :]
        * (pair_table.reshape(-1)[None, :] == block_ids[:, None]).astype(jnp.int32),
        axis=1,
    )
    span = window * block
    padded_docs = jnp.pad(doc_ids, ((0, 0), (span - block, 0)), constant_values=-1)
    padded_slots = jnp.pad(where_dealt, (window - 1, 0))
    slot_parts, bias_parts = [], []
    offset = jnp.arange(span, dtype=jnp.int32)
    for half in range(2):
        at = table_row[half]
        slot_parts.append(lax.dynamic_slice_in_dim(padded_slots, at, window, 0))
        key_doc = lax.dynamic_slice_in_dim(padded_docs, at * block, span, 1)
        query_doc = key_doc[:, span - block :]
        causal = offset[None, :] <= offset[:block, None] + (span - block)
        allowed = causal[None] & (key_doc[:, None, :] == query_doc[:, :, None])
        bias_parts.append(jnp.where(allowed, 0.0, masked_logits))
    slots = jnp.concatenate(slot_parts)
    owner, which = slots // 2, slots % 2
    lies = (owner % 2) * (2 * members) + (owner // 2 % 2) * members + owner // 4
    slots = jnp.concatenate([lies, which]).astype(jnp.int32)
    bias = jnp.stack(bias_parts, axis=1).reshape(2 * sequence_group, block, span).astype(F32)

    inputs = tokens.astype(F32)
    inv_one, normed_one = normalize(inputs)
    hidden_one = (normed_one * attn_gain_f).astype(BF16)
    query_lin = jnp.dot(hidden_one, query_full, preferred_element_type=F32).reshape(
        sequence_group, token_per_shard, QUERY_HEADS, HEAD_SIZE
    )
    key_linear = jnp.dot(hidden_one, key_full, preferred_element_type=F32).reshape(
        sequence_group, token_per_shard, KEY_VALUE_HEADS, HEAD_SIZE
    )
    value_rows = jnp.dot(hidden_one, value_full, preferred_element_type=F32).astype(BF16)
    query_rows = rotary_apply(query_lin, cosine_table, sine_table).astype(BF16)
    key_rows = (
        rotary_apply(key_linear, cosine_table, sine_table)
        .astype(BF16)
        .reshape(sequence_group, token_per_shard, KV_WIDTH)
    )
    own_kv = jnp.concatenate([key_rows, value_rows], axis=-1).reshape(
        2 * sequence_group, block, 2 * KV_WIDTH
    )
    flat_grad = out_grad.reshape(rows, width)
    kv_all, other_grad, output_full = gather_keys(
        members, own_kv, flat_grad, output_matrix
    )
    kv_all = kv_all.reshape(pairs, 2 * sequence_group, block, 2 * KV_WIDTH)

    query_parts = jnp.pad(to_groups(query_rows, block), ((0, 0), (0, 0), (0, 0), (0, KV_WIDTH)))
    mixed_parts, lse = attend(slots, query_parts, kv_all, bias, window, block)
    attn_in = from_groups(mixed_parts[..., KV_WIDTH:].astype(BF16), block)

    mixed_heads = inputs + jnp.dot(attn_in, output_full, preferred_element_type=F32)
    inv_two, normed_two = normalize(mixed_heads)
    hidden_two = (normed_two * mlp_gain_f).astype(BF16).reshape(rows, width)

    (other_hidden,) = swap_rows(members, 2, hidden_two)
    hid = jnp.concatenate([hidden_two, other_hidden])
    grads = jnp.concatenate([flat_grad, other_grad])
    gate = jnp.dot(hid, gate_matrix, preferred_element_type=F32)
    upper = jnp.dot(hid, up_matrix, preferred_element_type=F32)
    sigma = jax.nn.sigmoid(gate)
    activated = (gate * sigma * upper).astype(BF16)
    act_grad = back_dot(grads, down_matrix)
    up_grad_r = (act_grad * gate * sigma).astype(BF16)
    gate_grad_r = (act_grad * upper * sigma * (1.0 + gate * (1.0 - sigma))).astype(BF16)
    branch = jnp.dot(activated, down_matrix, preferred_element_type=F32)
    hidden_grad = back_dot(gate_grad_r, gate_matrix) + back_dot(up_grad_r, up_matrix)
    other_branch, other_hidden_grad = swap_rows(
        members, 3, branch[rows:].astype(BF16), hidden_grad[rows:].astype(BF16)
    )
    shape = (sequence_group, token_per_shard, width)
    branch_out = (branch[:rows] + other_branch.astype(F32)).reshape(shape)
    hidden_two_grad = (hidden_grad[:rows] + other_hidden_grad.astype(F32)).reshape(shape)
    units = gate_matrix.shape[1]
    gate_wgrad = chunks(outer_sum(gate_grad_r, hid).astype(BF16), members)
    up_wgrad = chunks(outer_sum(up_grad_r, hid).astype(BF16), members)
    down_wgrad = chunks(outer_sum(activated, grads).astype(BF16), members)

    block_out = (mixed_heads + branch_out).astype(BF16)
    mlp_gain_wgrad = jnp.sum(hidden_two_grad * normed_two, axis=(0, 1))
    mixed_grad = out_grad.astype(F32) + rms_back(
        hidden_two_grad * mlp_gain_f, inv_two, normed_two
    )
    branch_grad = mixed_grad.astype(BF16)
    attn_grad = back_dot(branch_grad, output_full).astype(BF16)
    grad_parts = jnp.pad(to_groups(attn_grad, block), ((0, 0), (0, 0), (0, 0), (KV_WIDTH, 0)))
    query_back, kv_back = attend_back(
        slots, query_parts, kv_all, bias, grad_parts, mixed_parts, lse, window, block
    )
    (kv_sum,) = reduce_chunks(
        members,
        4,
        ((("core", "x"), False),),
        (kv_back.reshape(2, 2, members, rows, 2 * KV_WIDTH),),
        rows // 2,
    )
    query_grad_r = (
        rotary_inverse(
            from_groups(query_back[..., :KV_WIDTH], block).reshape(
                sequence_group, token_per_shard, QUERY_HEADS, HEAD_SIZE
            ),
            cosine_table,
            sine_table,
        )
        .reshape(sequence_group, token_per_shard, QUERY_HEADS * HEAD_SIZE)
        .astype(BF16)
    )
    kv_sum = kv_sum.reshape(sequence_group, token_per_shard, 2 * KV_WIDTH)
    key_grad_r = (
        rotary_inverse(
            kv_sum[..., :KV_WIDTH].reshape(
                sequence_group, token_per_shard, KEY_VALUE_HEADS, HEAD_SIZE
            ),
            cosine_table,
            sine_table,
        )
        .reshape(sequence_group, token_per_shard, KV_WIDTH)
        .astype(BF16)
    )
    value_grad_r = kv_sum[..., KV_WIDTH:].astype(BF16)
    hidden_one_grad = (
        back_dot(query_grad_r, query_full)
        + back_dot(key_grad_r, key_full)
        + back_dot(value_grad_r, value_full)
    )
    attn_gain_wgrad = jnp.sum(hidden_one_grad * normed_one, axis=(0, 1))
    input_grad = mixed_grad + rms_back(hidden_one_grad * attn_gain_f, inv_one, normed_one)

    part = query_matrix.shape[0]
    qkv = jnp.concatenate([query_grad_r, key_grad_r, value_grad_r], axis=-1)
    qkv_wgrad = outer_sum(qkv, hidden_one).astype(BF16)
    output_wgrad = outer_sum(branch_grad, attn_in).astype(BF16)
    both = jnp.concatenate([qkv_wgrad, output_wgrad])
    count = both.shape[0] // 2
    sides = []
    for side in range(2):
        piece = both[:, side * part : (side + 1) * part]
        sides.append(chunks(jnp.concatenate([piece[:count], piece[count:]], axis=1), members))
    small = jnp.pad(jnp.stack([attn_gain_wgrad, mlp_gain_wgrad]), ((0, 6), (0, 0)))
    attn_total, gate_total, up_total, down_total, small_total = reduce_chunks(
        members,
        5,
        ((("core", "y", "x"), True),) + ((("core", "x"), True),) * 3,
        (jnp.stack(sides, axis=1), gate_wgrad, up_wgrad, down_wgrad),
        32,
        small,
    )
    flat = unchunk(attn_total, count)
    columns = jnp.concatenate([flat[:, :part], flat[:, part:]]).astype(F32)
    whole = columns.T
    kept = lax.dynamic_slice_in_dim(small_total, me_f * part, part, 1)
    heads = QUERY_HEADS * HEAD_SIZE
    return (
        block_out,
        input_grad,
        whole[:, :heads],
        whole[:, heads : heads + KV_WIDTH],
        whole[:, heads + KV_WIDTH : heads + 2 * KV_WIDTH],
        whole[:, heads + 2 * KV_WIDTH :],
        kept[0],
        kept[1],
        unchunk(gate_total, units).T.astype(F32),
        unchunk(up_total, units).T.astype(F32),
        unchunk(down_total, units).astype(F32),
    )


def solution(mesh):
    return jax.shard_map(
        body,
        mesh=mesh,
        in_specs=(
            P("fsdp", "ctx", None),
            P("fsdp", None),
            P("fsdp", None),
            P("fsdp", None),
            P("fsdp", None),
            P("fsdp"),
            P("fsdp"),
            P(None, "fsdp"),
            P(None, "fsdp"),
            P("fsdp", None),
            P(),
            P("fsdp", None),
            P("fsdp", "ctx", None),
        ),
        out_specs=(
            P("fsdp", "ctx", None),
            P("fsdp", "ctx", None),
            P("fsdp", None),
            P("fsdp", None),
            P("fsdp", None),
            P("fsdp", None),
            P("fsdp"),
            P("fsdp"),
            P(None, "fsdp"),
            P(None, "fsdp"),
            P("fsdp", None),
        ),
        check_vma=False,
    )
```

```python
import functools
import math

import jax
import jax.numpy as jnp
from jax import lax
from jax.experimental import pallas as pl
from jax.experimental.pallas import tpu as pltpu
from jax.sharding import PartitionSpec as P

QUERY_HEADS = 9
KEY_VALUE_HEADS = 3
HEAD_SIZE = 64
GROUP = QUERY_HEADS // KEY_VALUE_HEADS
KV_WIDTH = KEY_VALUE_HEADS * HEAD_SIZE
SCALE = 1.0 / math.sqrt(HEAD_SIZE)

epsilon = 1e-05
theta_base = 10000.0
masked_logits = -1e30

VMEM = pl.BlockSpec(memory_space=pltpu.VMEM)
SMEM = pl.BlockSpec(memory_space=pltpu.SMEM)
MESH = pl.DeviceIdType.MESH
F32 = jnp.float32
BF16 = jnp.bfloat16


class Place:
    def __init__(self, members):
        self.members = members
        self.ctx = lax.axis_index("ctx")
        self.fsdp = lax.axis_index("fsdp")
        self.core = self.ctx % 2
        self.x = (self.ctx // 2) % 2
        self.far = self.ctx // 4

    def own(self, axis):
        return {"core": self.core, "x": self.x, "y": self.fsdp}[axis]

    def partner(self, axis):
        if axis == "core":
            return (self.ctx + 1 - 2 * self.core, self.fsdp)
        if axis == "x":
            return (self.ctx + 2 - 4 * self.x, self.fsdp)
        return (self.ctx, 1 - self.fsdp)

    def far_member(self, step):
        return (self.far + step) % self.members

    def far_device(self, step):
        return (self.far_member(step) * 4 + self.ctx % 4, self.fsdp)

    def greet(self, axes, far):
        barrier = pltpu.get_barrier_semaphore()
        for axis in axes:
            pl.semaphore_signal(barrier, inc=1, device_id=self.partner(axis), device_id_type=MESH)
        count = len(axes)
        if far:
            for step in range(1, self.members):
                pl.semaphore_signal(
                    barrier, inc=1, device_id=self.far_device(step), device_id_type=MESH
                )
            count += self.members - 1
        pl.semaphore_wait(barrier, count)


class Sems:
    def __init__(self, send, recv):
        self.send, self.recv, self.at = send, recv, 0

    def copy(self, src, dst, device):
        at = self.at
        self.at += 1
        made = pltpu.make_async_remote_copy(
            src_ref=src,
            dst_ref=dst,
            send_sem=self.send.at[at],
            recv_sem=self.recv.at[at],
            device_id=device,
            device_id_type=MESH,
        )
        made.start()
        return made


def params(collective_id):
    return pltpu.CompilerParams(
        collective_id=collective_id, has_side_effects=True, vmem_limit_bytes=60 * 2**20
    )


def weights_kernel(members, count, *refs):
    ins, gain_in = refs[:count], refs[count]
    outs, gain_out = refs[count + 1 : 2 * count + 1], refs[2 * count + 1]
    send, recv = refs[2 * count + 2 :]
    me = Place(members)
    me.greet(("core", "y"), False)
    sems = Sems(send, recv)
    rows = ins[0].shape[0]
    half = rows // 2
    first = []
    for src, dst in zip(ins, outs):
        take = pl.ds(pl.multiple_of(me.core * half, 16), half)
        put = pl.ds(pl.multiple_of(me.fsdp * rows + me.core * half, 16), half)
        first.append(sems.copy(src.at[take], dst.at[put], me.partner("y")))
    gain = sems.copy(gain_in, gain_out.at[me.fsdp], me.partner("y"))
    gain_out[me.fsdp] = gain_in[...]
    for src, dst in zip(ins, outs):
        dst[pl.ds(pl.multiple_of(me.fsdp * rows, 16), rows)] = src[...]
    second = []
    for copy, dst in zip(first, outs):
        copy.wait_recv()
        put = pl.ds(pl.multiple_of((1 - me.fsdp) * rows + me.core * half, 16), half)
        second.append(sems.copy(dst.at[put], dst.at[put], me.partner("core")))
    for copy in second:
        copy.wait()
    for copy in first:
        copy.wait_send()
    gain.wait()


def gather_weights(members, weights, gains):
    count = len(weights)
    return pl.pallas_call(
        functools.partial(weights_kernel, members, count),
        out_shape=[jax.ShapeDtypeStruct((2 * w.shape[0], w.shape[1]), w.dtype) for w in weights]
        + [jax.ShapeDtypeStruct((2,) + gains.shape, gains.dtype)],
        in_specs=[VMEM] * (count + 1),
        out_specs=[VMEM] * (count + 1),
        scratch_shapes=[pltpu.SemaphoreType.DMA((2 * count + 1,))] * 2,
        compiler_params=params(0),
    )(*weights, gains)


def keys_kernel(
    members, kv_ref, grad_ref, w_ref, out_ref, other_ref, full_ref, send, recv
):
    me = Place(members)
    me.greet(("core", "x", "y"), True)
    sems = Sems(send, recv)
    rows = w_ref.shape[0]
    half = rows // 2
    mine = out_ref.at[me.core, me.x, me.far]
    far = [sems.copy(kv_ref, mine, me.far_device(step)) for step in range(1, members)]
    own = sems.copy(kv_ref, mine, me.partner("x"))
    put = pl.ds(pl.multiple_of(me.fsdp * rows + me.core * half, 16), half)
    weight = sems.copy(
        w_ref.at[pl.ds(pl.multiple_of(me.core * half, 16), half)],
        full_ref.at[put],
        me.partner("y"),
    )
    swap = sems.copy(grad_ref, other_ref, me.partner("y"))
    out_ref[me.core, me.x, me.far] = kv_ref[...]
    full_ref[pl.ds(pl.multiple_of(me.fsdp * rows, 16), rows)] = w_ref[...]
    along = []
    for step in range(1, members):
        far[step - 1].wait_recv()
        got = out_ref.at[me.core, me.x, me.far_member(members - step)]
        along.append(sems.copy(got, got, me.partner("x")))
    weight.wait_recv()
    put = pl.ds(pl.multiple_of((1 - me.fsdp) * rows + me.core * half, 16), half)
    across = sems.copy(full_ref.at[put], full_ref.at[put], me.partner("core"))
    block = out_ref.at[me.core, me.x]
    near = sems.copy(block, block, me.partner("core"))
    own.wait_recv()
    for copy in along:
        copy.wait_recv()
    block = out_ref.at[me.core, 1 - me.x]
    last = sems.copy(block, block, me.partner("core"))
    for copy in (near, last, across, swap):
        copy.wait()
    for copy in far + along + [own, weight]:
        copy.wait_send()


def gather_keys(members, kv, grad, weight):
    count = 2 * (members - 1) + 6
    return pl.pallas_call(
        functools.partial(keys_kernel, members),
        out_shape=[
            jax.ShapeDtypeStruct((2, 2, members) + kv.shape, kv.dtype),
            jax.ShapeDtypeStruct(grad.shape, grad.dtype),
            jax.ShapeDtypeStruct((2 * weight.shape[0], weight.shape[1]), weight.dtype),
        ],
        in_specs=[VMEM] * 3,
        out_specs=[VMEM] * 3,
        scratch_shapes=[pltpu.SemaphoreType.DMA((count,))] * 2,
        compiler_params=params(1),
    )(kv, grad, weight)


def swap_kernel(members, count, *refs):
    ins, outs = refs[:count], refs[count : 2 * count]
    send, recv = refs[2 * count :]
    me = Place(members)
    me.greet(("y",), False)
    sems = Sems(send, recv)
    copies = [sems.copy(src, dst, me.partner("y")) for src, dst in zip(ins, outs)]
    for copy in copies:
        copy.wait()


def swap_rows(members, collective_id, *arrays):
    count = len(arrays)
    return pl.pallas_call(
        functools.partial(swap_kernel, members, count),
        out_shape=[jax.ShapeDtypeStruct(a.shape, a.dtype) for a in arrays],
        in_specs=[VMEM] * count,
        out_specs=[VMEM] * count,
        scratch_shapes=[pltpu.SemaphoreType.DMA((count,))] * 2,
        compiler_params=params(collective_id),
    )(*arrays)


def add(a, b):
    return (a.astype(F32) + b.astype(F32)).astype(BF16)


def reduce_kernel(members, kinds, flows, has_small, *refs):
    refs = list(refs)
    ins = [refs.pop(0) for _ in kinds]
    small_in = refs.pop(0) if has_small else None
    outs = [refs.pop(0) for _ in kinds]
    small_out = refs.pop(0) if has_small else None
    gots = [[refs.pop(0) for _ in kinds[array][0]] for array, _, _ in flows]
    far_gots = [refs.pop(0) for _ in flows]
    axes_all = []
    for axes, _ in kinds:
        axes_all += [axis for axis in axes if axis not in axes_all]
    if has_small:
        small_acc, small_got, small_far = [refs.pop(0) for _ in range(3)]
    send, recv = refs
    me = Place(members)
    me.greet(tuple(axes_all), True)
    sems = Sems(send, recv)
    sent = []

    def go(src, dst, device):
        copy = sems.copy(src, dst, device)
        sent.append(copy)
        return copy

    def steps(f):
        array, low, rows = flows[f]
        axes, gather = kinds[array]
        cut = pl.ds(low, rows)

        def part(index):
            return ins[array].at[(index,) + (slice(None),) * len(axes) + (cut,)]

        flying = go(part(1 - me.own(axes[0])), gots[f][0], me.partner(axes[0]))
        yield
        for level, axis in enumerate(axes):
            flying.wait_recv()
            held = part(me.own(axis)) if level == 0 else gots[f][level - 1].at[me.own(axis)]
            got = gots[f][level]
            if level + 1 < len(axes):
                keep = me.own(axes[level + 1])
                away = 1 - keep
                got[away] = add(held[away], got[away])
                flying = go(got.at[away], gots[f][level + 1], me.partner(axes[level + 1]))
                got[keep] = add(held[keep], got[keep])
            else:
                spread_out = []
                for step in range(1, members):
                    to = me.far_member(step)
                    got[to] = add(held[to], got[to])
                    spread_out.append(
                        go(got.at[to], far_gots[f].at[step - 1], me.far_device(step))
                    )
                got[me.far] = add(held[me.far], got[me.far])
            yield
        whole = gots[f][-1][me.far].astype(F32)
        for step in range(1, members):
            spread_out[step - 1].wait_recv()
            whole = whole + far_gots[f][step - 1].astype(F32)
        if not gather:
            outs[array][cut] = whole
            return
        outs[array][me.core, me.x, me.far, cut] = whole.astype(BF16)
        mine = outs[array].at[me.core, me.x, me.far, cut]
        back = [go(mine, mine, me.far_device(step)) for step in range(1, members)]
        yield
        for copy in back:
            copy.wait_recv()
        block = outs[array].at[me.core, me.x, :, cut]
        flying = go(block, block, me.partner("x"))
        yield
        flying.wait_recv()
        block = outs[array].at[me.core, :, :, cut]
        flying = go(block, block, me.partner("core"))
        yield
        flying.wait_recv()

    def small_steps():
        depth = len(axes_all)
        small_acc[0] = small_in[...]
        for level in range(depth):
            flying = go(small_acc.at[level], small_got.at[level], me.partner(axes_all[level]))
            yield
            flying.wait_recv()
            small_acc[level + 1] = small_acc[level] + small_got[level]
        last = [
            go(small_acc.at[depth], small_far.at[step - 1], me.far_device(step))
            for step in range(1, members)
        ]
        yield
        whole = small_acc[depth]
        for step in range(1, members):
            last[step - 1].wait_recv()
            whole = whole + small_far[step - 1]
        small_out[...] = whole

    line = [steps(f) for f in range(len(flows))]
    starts = [max(0, f - 2) for f in range(len(flows))]
    if has_small:
        line.append(small_steps())
        starts.append(0)
    live, now = set(range(len(line))), 0
    while live:
        for f in sorted(live):
            if now >= starts[f] and next(line[f], True):
                live.discard(f)
        now += 1
    for copy in sent:
        copy.wait_send()


def reduce_chunks(members, collective_id, kinds, arrays, pieces, small=None):
    kinds = tuple((tuple(axes), gather) for axes, gather in kinds)
    outs, gots, fars, flows, count = [], [], [], [], 0
    for at, ((axes, gather), array) in enumerate(zip(kinds, arrays)):
        chunk = array.shape[len(axes) + 1 :]
        if gather:
            outs.append(jax.ShapeDtypeStruct((2, 2, members) + chunk, array.dtype))
        else:
            outs.append(jax.ShapeDtypeStruct(chunk, F32))
        low = 0
        while low < chunk[0]:
            rows = min(pieces, chunk[0] - low)
            flows.append((at, low, rows))
            low += rows
            for level in range(len(axes)):
                lead = array.shape[level + 1 : len(axes) + 1]
                gots.append(pltpu.VMEM(lead + (rows,) + chunk[1:], array.dtype))
            fars.append(pltpu.VMEM((members - 1, rows) + chunk[1:], array.dtype))
            count += len(axes) + members - 1 + (members + 1 if gather else 0)
    scratch = gots + fars
    operands = list(arrays)
    if small is not None:
        depth = max(len(axes) for axes, _ in kinds)
        outs.append(jax.ShapeDtypeStruct(small.shape, small.dtype))
        scratch += [
            pltpu.VMEM((depth + 1,) + small.shape, small.dtype),
            pltpu.VMEM((depth,) + small.shape, small.dtype),
            pltpu.VMEM((members - 1,) + small.shape, small.dtype),
        ]
        operands.append(small)
        count += depth + members - 1
    return pl.pallas_call(
        functools.partial(reduce_kernel, members, kinds, tuple(flows), small is not None),
        out_shape=outs,
        in_specs=[VMEM] * len(operands),
        out_specs=[VMEM] * len(outs),
        scratch_shapes=scratch + [pltpu.SemaphoreType.DMA((count,))] * 2,
        compiler_params=params(collective_id),
    )(*operands)


def lane_mask(base, head):
    lane = lax.broadcasted_iota(jnp.int32, (1, 2 * KV_WIDTH), 1)
    low = base + head * HEAD_SIZE
    return jnp.where((lane >= low) & (lane < low + HEAD_SIZE), 1.0, 0.0).astype(F32)


def spread(ref, part, base):
    rows = []
    for group in range(GROUP):
        value = ref[part, group].astype(F32)
        for head in range(KEY_VALUE_HEADS):
            rows.append(value * lane_mask(base, head))
    return jnp.concatenate(rows, axis=0)


def fold(value, base, out_ref, part, block):
    for group in range(GROUP):
        total = None
        for head in range(KEY_VALUE_HEADS):
            low = (group * KEY_VALUE_HEADS + head) * block
            piece = value[low : low + block] * lane_mask(base, head)
            total = piece if total is None else total + piece
        out_ref[part, group] = total


def key_window(kv_ref, slot_ref, half, seq, window):
    return jnp.concatenate(
        [
            kv_ref[slot_ref[half * window + j], seq * 2 + slot_ref[(2 + half) * window + j]]
            for j in range(window)
        ],
        axis=0,
    )


def nt(a, b):
    return lax.dot_general(a, b, (((1,), (1,)), ((), ())), preferred_element_type=F32)


def tn(a, b):
    return lax.dot_general(a, b, (((0,), (0,)), ((), ())), preferred_element_type=F32)


def attend_kernel(window, block, slot_ref, q_ref, kv_ref, bias_ref, out_ref, lse_ref):
    for seq in range(2):
        for half in range(2):
            part = seq * 2 + half
            keys = key_window(kv_ref, slot_ref, half, seq, window)
            query = spread(q_ref, part, 0).astype(BF16)
            bias = jnp.concatenate([bias_ref[part]] * QUERY_HEADS, axis=0)
            scores = nt(query, keys) * SCALE + bias
            top = jnp.max(scores, axis=-1, keepdims=True)
            weights = jnp.exp(scores - top)
            total = jnp.sum(weights, axis=-1, keepdims=True)
            probs = (weights / total).astype(BF16)
            mixed = jnp.dot(probs, keys, preferred_element_type=F32)
            fold(mixed, KV_WIDTH, out_ref, part, block)
            lse_ref[part] = top + jnp.log(total)


def attend(slots, query, kv, bias, window, block):
    return pl.pallas_call(
        functools.partial(attend_kernel, window, block),
        out_shape=[
            jax.ShapeDtypeStruct(query.shape, F32),
            jax.ShapeDtypeStruct((4, QUERY_HEADS * block, 1), F32),
        ],
        in_specs=[SMEM] + [VMEM] * 3,
        out_specs=[VMEM] * 2,
        compiler_params=pltpu.CompilerParams(vmem_limit_bytes=60 * 2**20),
    )(slots, query, kv, bias)


def attend_back_kernel(
    window, block, slot_ref, q_ref, kv_ref, bias_ref, grad_ref, o_ref, lse_ref, dq_ref, dkv_ref
):
    dkv_ref[...] = jnp.zeros_like(dkv_ref)
    for seq in range(2):
        for half in range(2):
            part = seq * 2 + half
            keys = key_window(kv_ref, slot_ref, half, seq, window)
            query = spread(q_ref, part, 0).astype(BF16)
            bias = jnp.concatenate([bias_ref[part]] * QUERY_HEADS, axis=0)
            probs = jnp.exp(nt(query, keys) * SCALE + bias - lse_ref[part])
            grad32 = spread(grad_ref, part, KV_WIDTH)
            mixed = spread(o_ref, part, KV_WIDTH)
            delta = jnp.sum(grad32 * mixed, axis=-1, keepdims=True)
            grad = grad32.astype(BF16)
            score_grad = (probs * (nt(grad, keys) - delta)).astype(BF16)
            fold(
                jnp.dot(score_grad, keys, preferred_element_type=F32) * SCALE,
                0,
                dq_ref,
                part,
                block,
            )
            back = tn(score_grad, query) * SCALE + tn(probs.astype(BF16), grad)
            for j in range(window):
                at = slot_ref[half * window + j]
                row = seq * 2 + slot_ref[(2 + half) * window + j]
                dkv_ref[at, row] = add(dkv_ref[at, row], back[j * block : (j + 1) * block])


def attend_back(slots, query, kv, bias, grad, mixed, lse, window, block):
    return pl.pallas_call(
        functools.partial(attend_back_kernel, window, block),
        out_shape=[
            jax.ShapeDtypeStruct(query.shape, F32),
            jax.ShapeDtypeStruct(kv.shape, kv.dtype),
        ],
        in_specs=[SMEM] + [VMEM] * 6,
        out_specs=[VMEM] * 2,
        compiler_params=pltpu.CompilerParams(vmem_limit_bytes=60 * 2**20),
    )(slots, query, kv, bias, grad, mixed, lse)


def rope_tables(token_positions):
    half = HEAD_SIZE // 2
    freq = theta_base ** (-jnp.arange(half, dtype=jnp.float32) * 2.0 / HEAD_SIZE)
    angles = token_positions.astype(jnp.float32)[:, None] * freq[None, :]
    cosine_table = jnp.concatenate([jnp.cos(angles), jnp.cos(angles)], axis=-1)
    sine_table = jnp.concatenate([jnp.sin(angles), jnp.sin(angles)], axis=-1)
    return (cosine_table[:, None, :], sine_table[:, None, :])


def rotary_apply(value_rows, cosine_table, sine_table):
    half = value_rows.shape[-1] // 2
    turned = jnp.concatenate([-value_rows[..., half:], value_rows[..., :half]], axis=-1)
    return value_rows * cosine_table + turned * sine_table


def rotary_inverse(grads, cosine_table, sine_table):
    half = grads.shape[-1] // 2
    scaled = grads * sine_table
    turned = jnp.concatenate([scaled[..., half:], -scaled[..., :half]], axis=-1)
    return grads * cosine_table + turned


def normalize(value_rows):
    inverse = lax.rsqrt(jnp.mean(value_rows * value_rows, axis=-1, keepdims=True) + epsilon)
    return (inverse, value_rows * inverse)


def rms_back(grads, inverse, normed):
    return inverse * (grads - normed * jnp.mean(grads * normed, axis=-1, keepdims=True))


def outer_sum(left, right):
    flat_left = left.reshape(-1, left.shape[-1])
    flat_right = right.reshape(-1, right.shape[-1])
    return lax.dot_general(
        flat_left, flat_right, (((0,), (0,)), ((), ())), preferred_element_type=jnp.float32
    )


def back_dot(grads, weight):
    return lax.dot_general(
        grads, weight, (((grads.ndim - 1,), (1,)), ((), ())), preferred_element_type=jnp.float32
    )


def to_groups(rows, block):
    split = rows.reshape(-1, block, KEY_VALUE_HEADS, GROUP, HEAD_SIZE)
    return jnp.transpose(split, (0, 3, 1, 2, 4)).reshape(-1, GROUP, block, KV_WIDTH)


def from_groups(parts, block):
    split = parts.reshape(-1, GROUP, block, KEY_VALUE_HEADS, HEAD_SIZE)
    return jnp.transpose(split, (0, 2, 3, 1, 4)).reshape(2, 2 * block, QUERY_HEADS * HEAD_SIZE)


def chunks(rows, members):
    count = 4 * members
    each = -(-rows.shape[0] // (count * 16)) * 16
    padded = jnp.pad(rows, ((0, count * each - rows.shape[0]), (0, 0)))
    return padded.reshape(2, 2, members, each, rows.shape[1])


def unchunk(array, rows):
    return array.reshape(-1, array.shape[-1])[:rows]


def body(
    tokens,
    query_matrix,
    key_projection,
    value_projection,
    output_matrix,
    attn_gain,
    mlp_gain,
    gate_matrix,
    up_matrix,
    down_matrix,
    pair_table,
    doc_ids,
    out_grad,
):
    sequence_group, token_per_shard, width = tokens.shape
    pairs = lax.axis_size("ctx")
    members = pairs // 4
    block = token_per_shard // 2
    length = token_per_shard * pairs
    blocks = 2 * pairs
    window = length // 8 // block + 1
    rows = sequence_group * token_per_shard
    me_f = lax.axis_index("fsdp")

    gains = jnp.pad(
        jnp.stack([attn_gain, mlp_gain]).astype(F32), ((0, 6), (0, 0))
    )
    query_full, key_full, value_full, gains_full = gather_weights(
        members, (query_matrix, key_projection, value_projection), gains
    )
    attn_gain_f = gains_full[:, 0].reshape(width)
    mlp_gain_f = gains_full[:, 1].reshape(width)

    table_row = lax.dynamic_index_in_dim(pair_table, lax.axis_index("ctx"), 0, keepdims=False)
    local = jnp.arange(token_per_shard, dtype=jnp.int32)
    own_pos = jnp.where(local < block, table_row[0], table_row[1]) * block + local % block
    cosine_table, sine_table = rope_tables(own_pos)

    block_ids = jnp.arange(blocks, dtype=jnp.int32)
    where_dealt = jnp.sum(
        block_ids[None, :]
        * (pair_table.reshape(-1)[None, :] == block_ids[:, None]).astype(jnp.int32),
        axis=1,
    )
    span = window * block
    padded_docs = jnp.pad(doc_ids, ((0, 0), (span - block, 0)), constant_values=-1)
    padded_slots = jnp.pad(where_dealt, (window - 1, 0))
    slot_parts, bias_parts = [], []
    offset = jnp.arange(span, dtype=jnp.int32)
    for half in range(2):
        at = table_row[half]
        slot_parts.append(lax.dynamic_slice_in_dim(padded_slots, at, window, 0))
        key_doc = lax.dynamic_slice_in_dim(padded_docs, at * block, span, 1)
        query_doc = key_doc[:, span - block :]
        causal = offset[None, :] <= offset[:block, None] + (span - block)
        allowed = causal[None] & (key_doc[:, None, :] == query_doc[:, :, None])
        bias_parts.append(jnp.where(allowed, 0.0, masked_logits))
    slots = jnp.concatenate(slot_parts)
    owner, which = slots // 2, slots % 2
    lies = (owner % 2) * (2 * members) + (owner // 2 % 2) * members + owner // 4
    slots = jnp.concatenate([lies, which]).astype(jnp.int32)
    bias = jnp.stack(bias_parts, axis=1).reshape(2 * sequence_group, block, span).astype(F32)

    inputs = tokens.astype(F32)
    inv_one, normed_one = normalize(inputs)
    hidden_one = (normed_one * attn_gain_f).astype(BF16)
    query_lin = jnp.dot(hidden_one, query_full, preferred_element_type=F32).reshape(
        sequence_group, token_per_shard, QUERY_HEADS, HEAD_SIZE
    )
    key_linear = jnp.dot(hidden_one, key_full, preferred_element_type=F32).reshape(
        sequence_group, token_per_shard, KEY_VALUE_HEADS, HEAD_SIZE
    )
    value_rows = jnp.dot(hidden_one, value_full, preferred_element_type=F32).astype(BF16)
    query_rows = rotary_apply(query_lin, cosine_table, sine_table).astype(BF16)
    key_rows = (
        rotary_apply(key_linear, cosine_table, sine_table)
        .astype(BF16)
        .reshape(sequence_group, token_per_shard, KV_WIDTH)
    )
    own_kv = jnp.concatenate([key_rows, value_rows], axis=-1).reshape(
        2 * sequence_group, block, 2 * KV_WIDTH
    )
    flat_grad = out_grad.reshape(rows, width)
    kv_all, other_grad, output_full = gather_keys(
        members, own_kv, flat_grad, output_matrix
    )
    kv_all = kv_all.reshape(pairs, 2 * sequence_group, block, 2 * KV_WIDTH)

    query_parts = jnp.pad(to_groups(query_rows, block), ((0, 0), (0, 0), (0, 0), (0, KV_WIDTH)))
    mixed_parts, lse = attend(slots, query_parts, kv_all, bias, window, block)
    attn_in = from_groups(mixed_parts[..., KV_WIDTH:].astype(BF16), block)

    mixed_heads = inputs + jnp.dot(attn_in, output_full, preferred_element_type=F32)
    inv_two, normed_two = normalize(mixed_heads)
    hidden_two = (normed_two * mlp_gain_f).astype(BF16).reshape(rows, width)

    (other_hidden,) = swap_rows(members, 2, hidden_two)
    hid = jnp.concatenate([hidden_two, other_hidden])
    grads = jnp.concatenate([flat_grad, other_grad])
    gate = jnp.dot(hid, gate_matrix, preferred_element_type=F32)
    upper = jnp.dot(hid, up_matrix, preferred_element_type=F32)
    sigma = jax.nn.sigmoid(gate)
    activated = (gate * sigma * upper).astype(BF16)
    act_grad = back_dot(grads, down_matrix)
    up_grad_r = (act_grad * gate * sigma).astype(BF16)
    gate_grad_r = (act_grad * upper * sigma * (1.0 + gate * (1.0 - sigma))).astype(BF16)
    branch = jnp.dot(activated, down_matrix, preferred_element_type=F32)
    hidden_grad = back_dot(gate_grad_r, gate_matrix) + back_dot(up_grad_r, up_matrix)
    other_branch, other_hidden_grad = swap_rows(
        members, 3, branch[rows:].astype(BF16), hidden_grad[rows:].astype(BF16)
    )
    shape = (sequence_group, token_per_shard, width)
    branch_out = (branch[:rows] + other_branch.astype(F32)).reshape(shape)
    hidden_two_grad = (hidden_grad[:rows] + other_hidden_grad.astype(F32)).reshape(shape)
    units = gate_matrix.shape[1]
    gate_wgrad = chunks(outer_sum(gate_grad_r, hid).astype(BF16), members)
    up_wgrad = chunks(outer_sum(up_grad_r, hid).astype(BF16), members)
    down_wgrad = chunks(outer_sum(activated, grads).astype(BF16), members)

    block_out = (mixed_heads + branch_out).astype(BF16)
    mlp_gain_wgrad = jnp.sum(hidden_two_grad * normed_two, axis=(0, 1))
    mixed_grad = out_grad.astype(F32) + rms_back(
        hidden_two_grad * mlp_gain_f, inv_two, normed_two
    )
    branch_grad = mixed_grad.astype(BF16)
    attn_grad = back_dot(branch_grad, output_full).astype(BF16)
    grad_parts = jnp.pad(to_groups(attn_grad, block), ((0, 0), (0, 0), (0, 0), (KV_WIDTH, 0)))
    query_back, kv_back = attend_back(
        slots, query_parts, kv_all, bias, grad_parts, mixed_parts, lse, window, block
    )
    (kv_sum,) = reduce_chunks(
        members,
        4,
        ((("core", "x"), False),),
        (kv_back.reshape(2, 2, members, rows, 2 * KV_WIDTH),),
        rows // 4,
    )
    query_grad_r = (
        rotary_inverse(
            from_groups(query_back[..., :KV_WIDTH], block).reshape(
                sequence_group, token_per_shard, QUERY_HEADS, HEAD_SIZE
            ),
            cosine_table,
            sine_table,
        )
        .reshape(sequence_group, token_per_shard, QUERY_HEADS * HEAD_SIZE)
        .astype(BF16)
    )
    kv_sum = kv_sum.reshape(sequence_group, token_per_shard, 2 * KV_WIDTH)
    key_grad_r = (
        rotary_inverse(
            kv_sum[..., :KV_WIDTH].reshape(
                sequence_group, token_per_shard, KEY_VALUE_HEADS, HEAD_SIZE
            ),
            cosine_table,
            sine_table,
        )
        .reshape(sequence_group, token_per_shard, KV_WIDTH)
        .astype(BF16)
    )
    value_grad_r = kv_sum[..., KV_WIDTH:].astype(BF16)
    hidden_one_grad = (
        back_dot(query_grad_r, query_full)
        + back_dot(key_grad_r, key_full)
        + back_dot(value_grad_r, value_full)
    )
    attn_gain_wgrad = jnp.sum(hidden_one_grad * normed_one, axis=(0, 1))
    input_grad = mixed_grad + rms_back(hidden_one_grad * attn_gain_f, inv_one, normed_one)

    part = query_matrix.shape[0]
    qkv = jnp.concatenate([query_grad_r, key_grad_r, value_grad_r], axis=-1)
    qkv_wgrad = outer_sum(qkv, hidden_one).astype(BF16)
    output_wgrad = outer_sum(branch_grad, attn_in).astype(BF16)
    both = jnp.concatenate([qkv_wgrad, output_wgrad])
    count = both.shape[0] // 2
    sides = []
    for side in range(2):
        piece = both[:, side * part : (side + 1) * part]
        sides.append(chunks(jnp.concatenate([piece[:count], piece[count:]], axis=1), members))
    small = jnp.pad(jnp.stack([attn_gain_wgrad, mlp_gain_wgrad]), ((0, 6), (0, 0)))
    attn_total, gate_total, up_total, down_total, small_total = reduce_chunks(
        members,
        5,
        ((("core", "y", "x"), True),) + ((("core", "x"), True),) * 3,
        (jnp.stack(sides, axis=1), gate_wgrad, up_wgrad, down_wgrad),
        16,
        small,
    )
    flat = unchunk(attn_total, count)
    columns = jnp.concatenate([flat[:, :part], flat[:, part:]]).astype(F32)
    whole = columns.T
    kept = lax.dynamic_slice_in_dim(small_total, me_f * part, part, 1)
    heads = QUERY_HEADS * HEAD_SIZE
    return (
        block_out,
        input_grad,
        whole[:, :heads],
        whole[:, heads : heads + KV_WIDTH],
        whole[:, heads + KV_WIDTH : heads + 2 * KV_WIDTH],
        whole[:, heads + 2 * KV_WIDTH :],
        kept[0],
        kept[1],
        unchunk(gate_total, units).T.astype(F32),
        unchunk(up_total, units).T.astype(F32),
        unchunk(down_total, units).astype(F32),
    )


def solution(mesh):
    return jax.shard_map(
        body,
        mesh=mesh,
        in_specs=(
            P("fsdp", "ctx", None),
            P("fsdp", None),
            P("fsdp", None),
            P("fsdp", None),
            P("fsdp", None),
            P("fsdp"),
            P("fsdp"),
            P(None, "fsdp"),
            P(None, "fsdp"),
            P("fsdp", None),
            P(),
            P("fsdp", None),
            P("fsdp", "ctx", None),
        ),
        out_specs=(
            P("fsdp", "ctx", None),
            P("fsdp", "ctx", None),
            P("fsdp", None),
            P("fsdp", None),
            P("fsdp", None),
            P("fsdp", None),
            P("fsdp"),
            P("fsdp"),
            P(None, "fsdp"),
            P(None, "fsdp"),
            P("fsdp", None),
        ),
        check_vma=False,
    )
```
